512 devices in a mesh: dp: 64 (over z, y), group: 8 (over x, core).
Axes of the slice: x: 4, y: 8, z: 8, core: 2. Of those that a mesh axis runs over, the one named last changes fastest.
Arguments:
- caption_tower_final_vectors: bfloat16 [2, 32768, 2048], P(None, ('dp', 'group')), may hold values from -6 to 6
- precomputed_picture_vectors: bfloat16 [16384, 1408], P('dp'), may hold values from -6 to 6
- pair_holder_rank: int32 [2, 32768, 1], P(None, ('dp', 'group')), may hold values from 0 to 63; in each aligned block of 64 rows (0 to 63, 64 to 127, ..., all dimensions but the last counted through in order) at most 2 rows name the same one
- pair_entry_position: int32 [2, 32768], P(None, ('dp', 'group')), may hold values from 0 to 255
- pair_targets: int32 [2, 32768], P(None, ('dp', 'group')), may hold values from 0 to 255
- picture_embedding_weights: bfloat16 [1408, 1024], P('dp'), may hold values from -0.15625 to 0.15625
- caption_embedding_weights: bfloat16 [2048, 1024], P('dp'), may hold values from -0.125 to 0.125
- score_stretch_learned: float32 [1], replicated, may hold values from 4 to 12
- sigmoid_offset_term: float32 [1], replicated, may hold values from -6 to -2
Outputs:
- text_grad: bfloat16 [2, 32768, 2048], P(None, ('dp', 'group'))
The draws below stay inside these ranges and needn't reach their ends.
Inputs may be any that keep to these rules, and one draw needn't show every extreme that they name: `pair_holder_rank`: among the 64 pairs of one device in one microbatch, at most 2 name the same owner, a bound that some block reaches.
All inputs are finite; a program needn't handle non-finite values.
Results may differ from the reference program's by a relative error of at most 0.007.
Values may be sent and summed in bfloat16 or wider, within the bound.
No kernel may reach another device: no remote copies, remote signals or barrier semaphores. Data moves between devices by JAX's collectives and lax.ppermute only.
A program may use at most 64 MiB of HBM per device.

```python
import math
import jax
import jax.numpy as jnp
import numpy as np
from jax import lax

D_IMG = 1408
D_TXT = 2048
EMB = 1024
MICRO = 2
PAIR_DEV = 64
CACHE_DEV = 256
CAP = 2
PAIRS = 32768
CACHE = 16384
NCLASS = 256
N_DP = 64
N_GROUP = 8


def plant(values, stream_key, least, high):
    longest = values.shape.index(max(values.shape))
    spots = []
    for shift in (0, 1):
        where = [jax.random.randint(jax.random.fold_in(stream_key, axis), (), 0, length) for axis, length in enumerate(values.shape)]
        where[longest] = (where[longest] + shift) % values.shape[longest]
        spots.append(tuple(where))
    return values.at[spots[0]].set(least).at[spots[1]].set(high)


def block_scale(stream_key, extent, pieces, least, top_value):
    gain = 1.0
    for dim, shards_of in pieces:
        draws = jax.random.uniform(jax.random.fold_in(jax.random.fold_in(stream_key, 6), dim), (shards_of,), jnp.float32, least / len(pieces), top_value / len(pieces))
        gain = gain * jnp.repeat(jnp.exp(draws), extent[dim] // shards_of).reshape((-1,) + (1,) * (len(extent) - 1 - dim))
    return gain


def routed_block(rng, own, number, rows, number_of, top, reach, skew):
    ranking = jax.random.permutation(rng, number_of)
    heavy_load, ordinary = shares(number_of, rows * top, reach, skew, True), shares(number_of, rows * top, reach, skew, False)
    places = jnp.arange(number_of)

    def named(lengths, turn):
        used = int((lengths > 0).sum())
        fixed = max(1, used // 4)
        moved = fixed + (places - fixed + turn * (used - fixed)) % max(1, number_of - fixed)
        return jnp.zeros((number_of,), jnp.int32).at[ranking[jnp.where(places < fixed, places, moved)]].set(jnp.asarray(lengths, jnp.int32))

    lengths = jnp.where(number % 4 == 0, named(heavy_load, number // 4), named(ordinary, number - number // 4 - 1))
    mixed = jax.random.permutation(jax.random.fold_in(own, 3), number_of)
    donor, receiver = mixed[0:number_of // 2 * 2:2], mixed[1:number_of // 2 * 2:2]
    margin = jnp.minimum(lengths[donor] - 1, reach - lengths[receiver]) // 2
    margin = jnp.where((donor == ranking[0]) | (receiver == ranking[0]) | (lengths[receiver] == 0), 0, jnp.maximum(margin, 0))
    moved = jax.random.randint(jax.random.fold_in(own, 4), (number_of // 2,), 0, 1 << 20) % (margin + 1)
    lengths = lengths.at[donor].add(-moved).at[receiver].add(moved)
    members = jnp.searchsorted(jnp.cumsum(lengths), jnp.arange(rows * top), side="right").astype(jnp.int32)
    table = members.reshape(top, rows).T
    table = table[jax.random.permutation(jax.random.fold_in(own, 1), rows)]
    turn = jax.random.randint(jax.random.fold_in(own, 2), (rows, 1), 0, top)
    return jnp.take_along_axis(table, (jnp.arange(top)[None, :] + turn) % top, axis=1)


def shares(amount, total, bound, skew, full):
    weights = [(1 << 20) // math.isqrt(rank ** skew) + 1 for rank in range(1, amount + 1)]
    largest = bound if full else min(bound, max(-(-total // amount), total * weights[0] // sum(weights)))
    least = 1 if total - largest >= amount - 1 else 0
    holding, spare = [largest] + [least] * (amount - 1), total - largest - least * (amount - 1)
    while spare > 0:
        free = [i for i in range(1, amount) if holding[i] < largest] or [i for i in range(1, amount) if holding[i] < bound]
        mass, budget = sum([weights[i] for i in free]), spare
        for i in free:
            extra = min(bound - holding[i], max(1, budget * weights[i] // mass), spare)
            holding[i] = holding[i] + extra
            spare = spare - extra
    return np.array(holding)


def noise(stream_key, extent, width, limit, split=(), held_as=jnp.bfloat16):
    level = block_scale(stream_key, extent, split, -0.22, 0.18) if split else 1.0
    array = jax.random.normal(stream_key, extent, jnp.float32) * width * level
    return jnp.minimum(jnp.maximum(array, -limit), limit).astype(held_as)


def setup_inputs(seed: int = 0) -> dict:
    splits = jax.random.split(jax.random.key(seed), 10)
    caption_tower_final_vectors = noise(splits[0], (MICRO, PAIRS, D_TXT), 1.0, 6.0, ((1, 512),))
    precomputed_picture_vectors = noise(splits[1], (CACHE, D_IMG), 1.0, 6.0, ((0, 64),))
    pair_holder_rank_keys = jax.random.split(jax.random.fold_in(splits[2], 1), MICRO * PAIRS // PAIR_DEV)
    pair_holder_rank_turns = jax.random.permutation(jax.random.fold_in(splits[2], 3), MICRO * PAIRS // PAIR_DEV)
    pair_holder_rank = jax.vmap(lambda own, number: routed_block(jax.random.fold_in(splits[2], 2), own, number, PAIR_DEV, N_DP, 1, CAP, 2))(pair_holder_rank_keys, pair_holder_rank_turns).reshape((MICRO, PAIRS, 1))
    pair_entry_position = plant(jax.random.randint(splits[3], (MICRO, PAIRS), 0, CACHE_DEV), jax.random.fold_in(splits[3], 1), 0, CACHE_DEV - 1).astype(jnp.int32)
    pair_targets = plant(jax.random.randint(splits[4], (MICRO, PAIRS), 0, NCLASS), jax.random.fold_in(splits[4], 1), 0, NCLASS - 1).astype(jnp.int32)
    picture_embedding_weights = noise(splits[5], (D_IMG, EMB), D_IMG ** -0.5, 0.15625, ((0, 64),))
    caption_embedding_weights = noise(splits[6], (D_TXT, EMB), D_TXT ** -0.5, 0.125, ((0, 64),))
    score_stretch_learned = jnp.clip(jnp.exp(jax.random.uniform(splits[7], (1,), jnp.float32, math.log(4.0), math.log(12.0))), 4.0, 12.0)
    sigmoid_offset_term = jnp.clip(jax.random.uniform(splits[8], (1,), jnp.float32, -6.0, -2.0), -6.0, -2.0)
    return {"caption_tower_final_vectors": caption_tower_final_vectors, "precomputed_picture_vectors": precomputed_picture_vectors, "pair_holder_rank": pair_holder_rank, "pair_entry_position": pair_entry_position, "pair_targets": pair_targets, "picture_embedding_weights": picture_embedding_weights, "caption_embedding_weights": caption_embedding_weights, "score_stretch_learned": score_stretch_learned, "sigmoid_offset_term": sigmoid_offset_term}


epsilon = 1e-06
loss_scale = 256.0

def unit_rows(values):
    inverse = lax.rsqrt(lax.optimization_barrier(jnp.sum(values * values, axis=-1, keepdims=True)) + epsilon)
    return (values * inverse, inverse)

def reference(caption_tower_final_vectors, precomputed_picture_vectors, pair_holder_rank, pair_entry_position, pair_targets, picture_embedding_weights, caption_embedding_weights, score_stretch_learned, sigmoid_offset_term):
    index_flat = (pair_holder_rank[..., 0] * CACHE_DEV + pair_entry_position).reshape(-1).astype(jnp.int32)
    features = precomputed_picture_vectors[index_flat]
    image_emb = unit_rows(jnp.dot(features, picture_embedding_weights, preferred_element_type=jnp.float32))[0].astype(jnp.bfloat16)
    group_size = N_GROUP * PAIR_DEV
    image_groups = image_emb.reshape(MICRO * N_DP, group_size, EMB)
    text_groups = caption_tower_final_vectors.reshape(MICRO * N_DP, group_size, D_TXT)
    label_groups = pair_targets.reshape(MICRO * N_DP, group_size)
    reciprocal_warmth_gain = score_stretch_learned[0]
    additive_displacement = sigmoid_offset_term[0]

    def one_group(inputs):
        text_rows, visual_frozen_encodings, group_labels = inputs
        text_raw = jnp.dot(text_rows, caption_embedding_weights, preferred_element_type=jnp.float32)
        text_unit, inverse = unit_rows(text_raw)
        sentence_encodings_halfwidth = text_unit.astype(jnp.bfloat16)
        pairwise_agreement_scores = reciprocal_warmth_gain * jnp.dot(sentence_encodings_halfwidth, visual_frozen_encodings.T, preferred_element_type=jnp.float32) + additive_displacement
        matched = (group_labels[:, None] == group_labels[None, :]).astype(jnp.float32)
        language_learned_parameters = (loss_scale * (jax.nn.sigmoid(pairwise_agreement_scores) - matched)).astype(jnp.bfloat16)
        descent_direction_vectors = reciprocal_warmth_gain * jnp.dot(language_learned_parameters, visual_frozen_encodings, preferred_element_type=jnp.float32)
        grad_raw = (inverse * (descent_direction_vectors - text_unit * lax.optimization_barrier(jnp.sum(text_unit * descent_direction_vectors, axis=-1, keepdims=True)))).astype(jnp.bfloat16)
        return jnp.dot(grad_raw, caption_embedding_weights.T, preferred_element_type=jnp.float32).astype(jnp.bfloat16)
    results = lax.map(one_group, (text_groups, image_groups, label_groups))
    return results.reshape(MICRO, PAIRS, D_TXT)
```

```python
import functools

import jax
import jax.numpy as jnp
from jax import lax
from jax.experimental import pallas as pl
from jax.experimental.pallas import tpu as pltpu
from jax.sharding import Mesh, PartitionSpec as P

EPS = 1e-06
LOSS_SCALE = 256.0
CAP = 2
LANES = 128
BF = jnp.bfloat16
F32 = jnp.float32
I32 = jnp.int32
VMEM = pl.BlockSpec(memory_space=pltpu.VMEM)
SMEM = pl.BlockSpec(memory_space=pltpu.SMEM)
ANY = pl.BlockSpec(memory_space=pl.ANY)
PARAMS = pltpu.CompilerParams(vmem_limit_bytes=40 * 1024 * 1024)


def dot(a, b, left, right):
    return lax.dot_general(a, b, (((left,), (right,)), ((), ())), preferred_element_type=F32)


def iota(shape, dim):
    return lax.broadcasted_iota(I32, shape, dim)


def as_column(row):
    return jnp.broadcast_to(row, (row.shape[1], row.shape[1])).T


def ask_kernel(micro, rows, owners, info, ask, slot):
    members = info.shape[0]
    pairs, slots = micro * rows, members * micro * CAP
    r, c = iota((pairs, pairs), 0), iota((pairs, pairs), 1)
    before = ((r < c) & ((r >= rows) == (c >= rows))).astype(F32).astype(BF)
    owner_id, slot_id = iota((owners, pairs), 0), iota((LANES, pairs), 0)
    half = (iota((1, pairs), 1) >= rows).astype(I32) * CAP
    total = jnp.zeros((owners, LANES), F32)
    for g in range(members):
        own, pos = info[g, 0:1, :], info[g, 1:2, :]
        hit = own == owner_id
        hits = hit.astype(F32)
        earlier = dot(hits.astype(BF), before, 1, 0)
        nth = jnp.sum(hits * earlier, axis=0, keepdims=True).astype(I32)
        place = g * micro * CAP + half + nth
        slot[g:g + 1, :] = own * slots + place
        put = jnp.where(place == slot_id, pos, 0).astype(F32).astype(BF)
        total = total + dot(hits.astype(BF), put, 1, 1)
    ask[...] = total.astype(BF)


def unsort_kernel(slot, fetched, mine):
    members, pairs = slot.shape
    count = fetched.shape[0]
    lane = iota((pairs, count), 1)
    for g in range(members):
        column = as_column(slot[g:g + 1, :])
        where = (lane == jnp.concatenate([column] * (count // pairs), axis=1)).astype(F32).astype(BF)
        mine[g * pairs:(g + 1) * pairs, :] = dot(where, fetched[...], 1, 0).astype(BF)


def load_columns(order, pieces, whole, sems):
    width = whole.shape[1] // len(pieces)
    copies = [
        pltpu.make_async_copy(
            piece, whole.at[:, pl.ds(pl.multiple_of(order[k] * width, LANES), width)], sems.at[k]
        )
        for k, piece in enumerate(pieces)
    ]
    for copy in copies:
        copy.start()
    return copies


def text_kernel(members, order, text, *refs):
    pieces, (unit, inverse, wt, sems) = refs[:members], refs[members:]
    for copy in load_columns(order, pieces, wt, sems):
        copy.wait()
    raw = dot(text[...], wt[...], 1, 0)
    inv = lax.rsqrt(jnp.sum(raw * raw, axis=1, keepdims=True) + EPS)
    unit[...] = raw * inv
    inverse[...] = jnp.broadcast_to(inv, inverse.shape)


def grad_kernel(members, rows, order, scalars, info, labels, unit, inverse, *refs):
    images, weights = refs[:members], refs[members:2 * members]
    out, img, wt, slopes, img_sems, wt_sems = refs[2 * members:]
    img_copies = load_columns(order, images, img, img_sems)
    wt_copies = load_columns(order, weights, wt, wt_sems)
    gain, offset = scalars[0], scalars[1]
    pairs = unit.shape[0]
    text = unit[...].astype(BF)
    same_micro = (iota((pairs, pairs), 0) >= rows) == (iota((pairs, pairs), 1) >= rows)
    for copy in img_copies:
        copy.wait()
    for g in range(members):
        span = slice(g * pairs, (g + 1) * pairs)
        block = img[span, :]
        wide = block.astype(F32)
        inv = lax.rsqrt(jnp.sum(wide * wide, axis=1, keepdims=True) + EPS)
        logit = gain * inv * dot(block, text, 1, 1) + offset
        match = (as_column(info[g, 2:3, :]) == labels[...]).astype(F32)
        slope = LOSS_SCALE * inv * (jax.nn.sigmoid(logit) - match)
        slopes[span, :] = jnp.where(same_micro, slope, 0.0).astype(BF)
    grad = gain * dot(slopes[...], img[...], 0, 0)
    grad = grad - unit[...] * jnp.sum(unit[...] * grad, axis=1, keepdims=True)
    grad = (inverse[:, 0:1] * grad).astype(BF)
    for copy in wt_copies:
        copy.wait()
    out[...] = dot(grad, wt[...], 1, 1).astype(BF)


def make_local(nz, ny, nx, nc):
    members, owners = nx * nc, nz * ny

    def swap(v):
        return lax.ppermute(v, "core", [(i, nc - 1 - i) for i in range(nc)])

    def shift(v, by):
        return lax.ppermute(v, "x", [(i, (i + by) % nx) for i in range(nx)])

    def turn(v):
        moves = [(i * nc + c, (i + (1 if c == 0 else -1)) % nx * nc + c) for i in range(nx) for c in range(nc)]
        return lax.ppermute(v, ("x", "core"), moves)

    def whole_group(v, core):
        up, down = shift(v, 1), shift(v, -1)
        far = turn(jnp.where(core == 0, up, down))
        near = [v, up, far, down]
        return near + [swap(p) for p in near]

    def local(text, cache, owner, entry, labels, wi, wt, stretch, offset):
        micro, rows, d_txt = text.shape
        d_img, emb = cache.shape[1], wi.shape[1]
        wi_rows, wt_rows = wi.shape[0], wt.shape[0]
        width = emb // members
        pairs = micro * rows
        slots = members * micro * CAP
        x, core = lax.axis_index("x"), lax.axis_index("core")
        me = x * nc + core
        order = jnp.stack([(x - k) % nx * nc + (core ^ d) for d in range(nc) for k in range(nx)])

        info = jnp.stack([owner.reshape(pairs), entry.reshape(pairs), labels.reshape(pairs)])
        info = jnp.broadcast_to(info[None], (members,) + info.shape)
        info = lax.all_to_all(info, ("x", "core"), split_axis=0, concat_axis=0, tiled=True)
        ask, slot = pl.pallas_call(
            functools.partial(ask_kernel, micro, rows, owners),
            out_shape=(
                jax.ShapeDtypeStruct((owners, LANES), BF),
                jax.ShapeDtypeStruct((members, pairs), I32),
            ),
            in_specs=[VMEM],
            out_specs=(VMEM, VMEM),
            compiler_params=PARAMS,
        )(info)

        wi_pad = -(-(wi_rows + 1) // 8) * 8
        wt_part = lax.dynamic_slice(wt, (0, me * width), (wt_rows, width))
        wi_part = lax.dynamic_slice(wi, (0, me * width), (wi_rows, width))
        fixed = jnp.concatenate([wt_part, wi_part], axis=0)
        sent = jnp.concatenate(
            [
                jnp.broadcast_to(fixed[None], (owners,) + fixed.shape),
                ask[:, None, :],
                jnp.zeros((owners, wi_pad - wi_rows - 1, width), BF),
            ],
            axis=1,
        )
        got = lax.all_to_all(sent, ("z", "y"), split_axis=0, concat_axis=0, tiled=True)

        old, new = iota((d_img, owners * wi_pad), 0), iota((d_img, owners * wi_pad), 1)
        spread = (old // wi_rows * wi_pad + old % wi_rows == new).astype(BF)
        cache_pad = dot(cache, spread, 1, 0).astype(BF)
        wi_all = got[:, wt_rows:].reshape(owners * wi_pad, width)
        table = dot(cache_pad, wi_all, 1, 0).astype(BF)
        asked = got[:, wt_rows + wi_rows, :slots].astype(I32).reshape(-1)
        pick = (asked[:, None] == jnp.arange(cache.shape[0], dtype=I32)).astype(BF)
        served = dot(pick, table, 1, 0).astype(BF).reshape(owners, slots, width)
        fetched = lax.all_to_all(served, ("z", "y"), split_axis=0, concat_axis=0, tiled=True)
        mine = pl.pallas_call(
            unsort_kernel,
            out_shape=jax.ShapeDtypeStruct((members * pairs, width), BF),
            in_specs=[VMEM, VMEM],
            out_specs=VMEM,
            compiler_params=PARAMS,
        )(slot, fetched.reshape(owners * slots, width))

        wt_pieces = whole_group(got[:, :wt_rows].reshape(owners * wt_rows, width), core)
        unit, inverse = pl.pallas_call(
            functools.partial(text_kernel, members),
            out_shape=(
                jax.ShapeDtypeStruct((pairs, emb), F32),
                jax.ShapeDtypeStruct((pairs, LANES), F32),
            ),
            in_specs=[SMEM, VMEM] + [ANY] * members,
            out_specs=(VMEM, VMEM),
            scratch_shapes=[
                pltpu.VMEM((d_txt, emb), BF),
                pltpu.SemaphoreType.DMA((members,)),
            ],
            compiler_params=PARAMS,
            cost_estimate=pl.CostEstimate(
                flops=2 * pairs * d_txt * emb, bytes_accessed=2 * d_txt * emb, transcendentals=0
            ),
        )(order, text.reshape(pairs, d_txt), *wt_pieces)

        image_pieces = whole_group(mine, core)
        out = pl.pallas_call(
            functools.partial(grad_kernel, members, rows),
            out_shape=jax.ShapeDtypeStruct((pairs, d_txt), BF),
            in_specs=[SMEM, SMEM, VMEM, VMEM, VMEM, VMEM] + [ANY] * (2 * members),
            out_specs=VMEM,
            scratch_shapes=[
                pltpu.VMEM((members * pairs, emb), BF),
                pltpu.VMEM((d_txt, emb), BF),
                pltpu.VMEM((members * pairs, pairs), BF),
                pltpu.SemaphoreType.DMA((members,)),
                pltpu.SemaphoreType.DMA((members,)),
            ],
            compiler_params=PARAMS,
            cost_estimate=pl.CostEstimate(
                flops=2 * pairs * d_txt * emb, bytes_accessed=2 * d_txt * emb, transcendentals=0
            ),
        )(
            order,
            jnp.concatenate([stretch, offset]),
            info,
            labels.reshape(1, pairs),
            unit,
            inverse,
            *image_pieces,
            *wt_pieces,
        )
        return out.reshape(micro, rows, d_txt)

    return local


def solution(mesh):
    nz, ny, nx, nc = 8, 8, 4, 2
    fine = Mesh(mesh.devices.reshape(nz, ny, nx, nc), ("z", "y", "x", "core"))
    dp, every = ("z", "y"), ("z", "y", "x", "core")
    return jax.shard_map(
        make_local(nz, ny, nx, nc),
        mesh=fine,
        in_specs=(
            P(None, every, None),
            P(dp, None),
            P(None, every, None),
            P(None, every),
            P(None, every),
            P(dp, None),
            P(dp, None),
            P(),
            P(),
        ),
        out_specs=P(None, every, None),
        check_vma=False,
    )
```

```python
import functools

import jax
import jax.numpy as jnp
from jax import lax
from jax.experimental import pallas as pl
from jax.experimental.pallas import tpu as pltpu
from jax.sharding import Mesh, PartitionSpec as P

EPS = 1e-06
LOSS_SCALE = 256.0
CAP = 2
LANES = 128
BF = jnp.bfloat16
F32 = jnp.float32
I32 = jnp.int32
VMEM = pl.BlockSpec(memory_space=pltpu.VMEM)
SMEM = pl.BlockSpec(memory_space=pltpu.SMEM)
ANY = pl.BlockSpec(memory_space=pl.ANY)
HBM = pl.BlockSpec(memory_space=pltpu.HBM)
PARAMS = pltpu.CompilerParams(vmem_limit_bytes=24 * 1024 * 1024)
SMALL = pltpu.CompilerParams(vmem_limit_bytes=16 * 1024 * 1024)
LARGE = pltpu.CompilerParams(vmem_limit_bytes=58 * 1024 * 1024)


def dot(a, b, left, right):
    return lax.dot_general(a, b, (((left,), (right,)), ((), ())), preferred_element_type=F32)


def iota(shape, dim):
    return lax.broadcasted_iota(I32, shape, dim)


def as_column(row):
    return jnp.broadcast_to(row, (row.shape[1], row.shape[1])).T


def pack_kernel(owner, entry, labels, info):
    micro = owner.shape[0]
    lines = [
        [owner[m] for m in range(micro)],
        [entry[m:m + 1, :] for m in range(micro)],
        [labels[m:m + 1, :] for m in range(micro)],
    ]
    for k, line in enumerate(lines):
        line = jnp.concatenate(line, axis=1)
        info[0, k:k + 1, :] = line


def ask_kernel(micro, rows, owners, info, ask, slot):
    members = info.shape[0]
    pairs, slots = micro * rows, members * micro * CAP
    r, c = iota((pairs, pairs), 0), iota((pairs, pairs), 1)
    before = ((r < c) & ((r >= rows) == (c >= rows))).astype(F32).astype(BF)
    owner_id, slot_id = iota((owners, pairs), 0), iota((LANES, pairs), 0)
    half = (iota((1, pairs), 1) >= rows).astype(I32) * CAP
    total = jnp.zeros((owners, LANES), F32)
    for g in range(members):
        own, pos = info[g, 0:1, :], info[g, 1:2, :]
        hit = own == owner_id
        hits = hit.astype(F32)
        earlier = dot(hits.astype(BF), before, 1, 0)
        nth = jnp.sum(hits * earlier, axis=0, keepdims=True).astype(I32)
        place = g * micro * CAP + half + nth
        slot[g:g + 1, :] = own * slots + place
        put = jnp.where(place == slot_id, pos, 0).astype(F32).astype(BF)
        total = total + dot(hits.astype(BF), put, 1, 1)
    ask[...] = total.astype(BF)


def unsort_kernel(me, slot, fetched, mine):
    members, pairs = slot.shape
    count = fetched.shape[0]
    lane = iota((pairs, count), 1)
    for g in range(members):
        column = as_column(slot[g:g + 1, :])
        where = (lane == jnp.concatenate([column] * (count // pairs), axis=1)).astype(F32).astype(BF)
        start = pl.multiple_of((me[0] ^ g) * pairs, pairs)
        mine[pl.ds(start, pairs), :] = dot(where, fetched[...], 1, 0).astype(BF)


def load_columns(me, cores, pieces, whole, sems):
    chips, width = len(pieces) // cores, whole.shape[1] // len(pieces)
    x, core = me // cores, me % cores
    copies = []
    for k, piece in enumerate(pieces):
        member = (x + chips - k % chips) % chips * cores + (core ^ (k // chips))
        columns = pl.ds(pl.multiple_of(member * width, LANES), width)
        copies.append(pltpu.make_async_copy(piece, whole.at[:, columns], sems.at[k]))
    for copy in copies:
        copy.start()
    return copies


def text_kernel(members, cores, me, text, *refs):
    pieces, (unit, inverse, whole, wt, unit_buf, sems, out_sems) = refs[:members], refs[members:]
    for copy in load_columns(me[0], cores, pieces, wt, sems):
        copy.wait()
    wt_out = pltpu.make_async_copy(wt, whole, out_sems.at[0])
    wt_out.start()
    raw = dot(text[...], wt[...], 1, 0)
    inv = lax.rsqrt(jnp.sum(raw * raw, axis=1, keepdims=True) + EPS)
    unit_buf[...] = raw * inv
    unit_out = pltpu.make_async_copy(unit_buf, unit, out_sems.at[1])
    unit_out.start()
    inverse[...] = jnp.broadcast_to(inv, inverse.shape)
    wt_out.wait()
    unit_out.wait()


def grad_kernel(members, cores, rows, me, stretch, shift, info, inverse, unit_in, weights, *refs):
    images, (out, img, wt, unit, slopes, img_sems, sems) = refs[:members], refs[members:]
    unit_copy = pltpu.make_async_copy(unit_in, unit, sems.at[0])
    unit_copy.start()
    img_copies = load_columns(me[0], cores, images, img, img_sems)
    wt_copy = pltpu.make_async_copy(weights, wt, sems.at[1])
    wt_copy.start()
    gain, offset = stretch[0], shift[0]
    pairs = unit.shape[0]
    unit_copy.wait()
    text = unit[...].astype(BF)
    own_labels = info[0, 2:3, :]
    same_micro = (iota((pairs, pairs), 0) >= rows) == (iota((pairs, pairs), 1) >= rows)
    for copy in img_copies:
        copy.wait()
    for g in range(members):
        span = slice(g * pairs, (g + 1) * pairs)
        block = img[span, :]
        wide = block.astype(F32)
        inv = lax.rsqrt(jnp.sum(wide * wide, axis=1, keepdims=True) + EPS)
        logit = gain * inv * dot(block, text, 1, 1) + offset
        match = (as_column(info[me[0] ^ g, 2:3, :]) == own_labels).astype(F32)
        slope = LOSS_SCALE * inv * (jax.nn.sigmoid(logit) - match)
        slopes[span, :] = jnp.where(same_micro, slope, 0.0).astype(BF)
    grad = gain * dot(slopes[...], img[...], 0, 0)
    grad = grad - unit[...] * jnp.sum(unit[...] * grad, axis=1, keepdims=True)
    grad = (inverse[:, 0:1] * grad).astype(BF)
    wt_copy.wait()
    out[...] = dot(grad, wt[...], 1, 1).astype(BF)


def make_local(nz, ny, nx, nc):
    members, owners = nx * nc, nz * ny

    def swap(v):
        return lax.ppermute(v, "core", [(i, nc - 1 - i) for i in range(nc)])

    def double(v, axis, bit):
        size = lax.axis_size(axis)
        other = lax.ppermute(v, axis, [(i, i ^ (1 << bit)) for i in range(size)])
        return jnp.concatenate([v, other], axis=0)

    def shift(v, by):
        return lax.ppermute(v, "x", [(i, (i + by) % nx) for i in range(nx)])

    def turn(v):
        moves = [(i * nc + c, (i + 1 - 2 * c) % nx * nc + c) for i in range(nx) for c in range(nc)]
        return lax.ppermute(v, ("x", "core"), moves)

    def whole_group(v, core):
        up, down = shift(v, 1), shift(v, -1)
        twin = swap(v)
        far = turn(jnp.where(core == 0, up, down))
        return [v, up, far, down, twin, swap(up), swap(far), swap(down)]

    def local(text, cache, owner, entry, labels, wi, wt, stretch, offset):
        micro, rows, d_txt = text.shape
        d_img, emb = cache.shape[1], wi.shape[1]
        wi_rows, wt_rows = wi.shape[0], wt.shape[0]
        width = emb // members
        pairs = micro * rows
        slots = members * micro * CAP
        x, core = lax.axis_index("x"), lax.axis_index("core")
        me = x * nc + core

        wt_part = lax.dynamic_slice(wt, (0, me * width), (wt_rows, width))
        wt_part = jnp.broadcast_to(wt_part[None], (owners,) + wt_part.shape)
        wt_part = lax.all_to_all(wt_part, ("z", "y"), split_axis=0, concat_axis=0, tiled=True)
        wt_part = wt_part.reshape(owners * wt_rows, width)
        info = pl.pallas_call(
            pack_kernel,
            out_shape=jax.ShapeDtypeStruct((1, 3, pairs), I32),
            in_specs=[VMEM, VMEM, VMEM],
            out_specs=VMEM,
            compiler_params=LARGE,
        )(owner.transpose(0, 2, 1), entry, labels)
        info = double(double(double(info, "core", 0), "x", 0), "x", 1)
        info, wt_part = lax.optimization_barrier((info, wt_part))
        wt_pieces = whole_group(wt_part, core)
        ask, slot = pl.pallas_call(
            functools.partial(ask_kernel, micro, rows, owners),
            out_shape=(
                jax.ShapeDtypeStruct((owners, LANES), BF),
                jax.ShapeDtypeStruct((members, pairs), I32),
            ),
            in_specs=[VMEM],
            out_specs=(VMEM, VMEM),
            compiler_params=SMALL,
        )(info)

        wi_pad = -(-(wi_rows + 1) // 8) * 8
        wi_part = lax.dynamic_slice(wi, (0, me * width), (wi_rows, width))
        sent = jnp.concatenate(
            [
                jnp.broadcast_to(wi_part[None], (owners,) + wi_part.shape),
                ask[:, None, :],
                jnp.zeros((owners, wi_pad - wi_rows - 1, width), BF),
            ],
            axis=1,
        )
        got = lax.all_to_all(sent, ("z", "y"), split_axis=0, concat_axis=0, tiled=True)

        old, new = iota((d_img, owners * wi_pad), 0), iota((d_img, owners * wi_pad), 1)
        spread = (old // wi_rows * wi_pad + old % wi_rows == new).astype(BF)
        cache_pad = dot(cache, spread, 1, 0).astype(BF)
        wi_all = got.reshape(owners * wi_pad, width)
        table = dot(cache_pad, wi_all, 1, 0).astype(BF)
        asked = got[:, wi_rows, :slots].astype(I32).reshape(-1)
        pick = (asked[:, None] == jnp.arange(cache.shape[0], dtype=I32)).astype(BF)
        served = dot(pick, table, 1, 0).astype(BF).reshape(owners, slots, width)
        fetched = lax.all_to_all(served, ("z", "y"), split_axis=0, concat_axis=0, tiled=True)
        unit, inverse, wt_whole = pl.pallas_call(
            functools.partial(text_kernel, members, nc),
            out_shape=(
                jax.ShapeDtypeStruct((pairs, emb), F32),
                jax.ShapeDtypeStruct((pairs, LANES), F32),
                jax.ShapeDtypeStruct((d_txt, emb), BF),
            ),
            in_specs=[SMEM, VMEM] + [ANY] * members,
            out_specs=(HBM, VMEM, HBM),
            scratch_shapes=[
                pltpu.VMEM((d_txt, emb), BF),
                pltpu.VMEM((pairs, emb), F32),
                pltpu.SemaphoreType.DMA((members,)),
                pltpu.SemaphoreType.DMA((2,)),
            ],
            compiler_params=PARAMS,
            cost_estimate=pl.CostEstimate(
                flops=2 * pairs * d_txt * emb, bytes_accessed=4 * d_txt * emb, transcendentals=0
            ),
        )(me.reshape(1), text.reshape(pairs, d_txt), *wt_pieces)
        fetched, unit, inverse, wt_whole = lax.optimization_barrier((fetched, unit, inverse, wt_whole))
        mine = pl.pallas_call(
            unsort_kernel,
            out_shape=jax.ShapeDtypeStruct((members * pairs, width), BF),
            in_specs=[SMEM, VMEM, VMEM],
            out_specs=VMEM,
            compiler_params=SMALL,
        )(me.reshape(1), slot, fetched.reshape(owners * slots, width))

        image_pieces = whole_group(mine, core)
        out = pl.pallas_call(
            functools.partial(grad_kernel, members, nc, rows),
            out_shape=jax.ShapeDtypeStruct((pairs, d_txt), BF),
            in_specs=[SMEM, SMEM, SMEM, VMEM, VMEM, HBM, HBM] + [ANY] * members,
            out_specs=VMEM,
            scratch_shapes=[
                pltpu.VMEM((members * pairs, emb), BF),
                pltpu.VMEM((d_txt, emb), BF),
                pltpu.VMEM((pairs, emb), F32),
                pltpu.VMEM((members * pairs, pairs), BF),
                pltpu.SemaphoreType.DMA((members,)),
                pltpu.SemaphoreType.DMA((2,)),
            ],
            compiler_params=LARGE,
            cost_estimate=pl.CostEstimate(
                flops=2 * pairs * d_txt * emb, bytes_accessed=2 * d_txt * emb, transcendentals=0
            ),
        )(me.reshape(1), stretch, offset, info, inverse, unit, wt_whole, *image_pieces)
        return out.reshape(micro, rows, d_txt)

    return local


def solution(mesh):
    nz, ny, nx, nc = 8, 8, 4, 2
    fine = Mesh(mesh.devices.reshape(nz, ny, nx, nc), ("z", "y", "x", "core"))
    dp, every = ("z", "y"), ("z", "y", "x", "core")
    return jax.shard_map(
        make_local(nz, ny, nx, nc),
        mesh=fine,
        in_specs=(
            P(None, every, None),
            P(dp, None),
            P(None, every, None),
            P(None, every),
            P(None, every),
            P(dp, None),
            P(dp, None),
            P(),
            P(),
        ),
        out_specs=P(None, every, None),
        check_vma=False,
    )
```

```python
import functools

import jax
import jax.numpy as jnp
from jax import lax
from jax.experimental import pallas as pl
from jax.experimental.pallas import tpu as pltpu
from jax.sharding import Mesh, PartitionSpec as P

EPS = 1e-06
LOSS_SCALE = 256.0
CAP = 2
LANES = 128
BF = jnp.bfloat16
F32 = jnp.float32
I32 = jnp.int32
VMEM = pl.BlockSpec(memory_space=pltpu.VMEM)
SMEM = pl.BlockSpec(memory_space=pltpu.SMEM)
ANY = pl.BlockSpec(memory_space=pl.ANY)
SMALL = pltpu.CompilerParams(vmem_limit_bytes=16 * 1024 * 1024)
LARGE = pltpu.CompilerParams(vmem_limit_bytes=58 * 1024 * 1024)


def dot(a, b, left, right):
    return lax.dot_general(a, b, (((left,), (right,)), ((), ())), preferred_element_type=F32)


def iota(shape, dim):
    return lax.broadcasted_iota(I32, shape, dim)


def as_column(row):
    return jnp.broadcast_to(row, (row.shape[1], row.shape[1])).T


def pack_kernel(owner, entry, labels, info):
    micro = owner.shape[0]
    lines = [
        [owner[m] for m in range(micro)],
        [entry[m:m + 1, :] for m in range(micro)],
        [labels[m:m + 1, :] for m in range(micro)],
    ]
    for k, line in enumerate(lines):
        line = jnp.concatenate(line, axis=1)
        for g in range(info.shape[0]):
            info[g, k:k + 1, :] = line


def ask_kernel(micro, rows, owners, info, ask, slot):
    members = info.shape[0]
    pairs, slots = micro * rows, members * micro * CAP
    r, c = iota((pairs, pairs), 0), iota((pairs, pairs), 1)
    before = ((r < c) & ((r >= rows) == (c >= rows))).astype(F32).astype(BF)
    owner_id, slot_id = iota((owners, pairs), 0), iota((LANES, pairs), 0)
    half = (iota((1, pairs), 1) >= rows).astype(I32) * CAP
    total = jnp.zeros((owners, LANES), F32)
    for g in range(members):
        own, pos = info[g, 0:1, :], info[g, 1:2, :]
        hit = own == owner_id
        hits = hit.astype(F32)
        earlier = dot(hits.astype(BF), before, 1, 0)
        nth = jnp.sum(hits * earlier, axis=0, keepdims=True).astype(I32)
        place = g * micro * CAP + half + nth
        slot[g:g + 1, :] = own * slots + place
        put = jnp.where(place == slot_id, pos, 0).astype(F32).astype(BF)
        total = total + dot(hits.astype(BF), put, 1, 1)
    ask[...] = total.astype(BF)


def unsort_kernel(slot, fetched, mine):
    members, pairs = slot.shape
    count = fetched.shape[0]
    lane = iota((pairs, count), 1)
    for g in range(members):
        column = as_column(slot[g:g + 1, :])
        where = (lane == jnp.concatenate([column] * (count // pairs), axis=1)).astype(F32).astype(BF)
        mine[g * pairs:(g + 1) * pairs, :] = dot(where, fetched[...], 1, 0).astype(BF)


def load_columns(me, cores, pieces, whole, sems):
    chips, width = len(pieces) // cores, whole.shape[1] // len(pieces)
    x, core = me // cores, me % cores
    copies = []
    for k, piece in enumerate(pieces):
        member = (x + chips - k % chips) % chips * cores + (core ^ (k // chips))
        columns = pl.ds(pl.multiple_of(member * width, LANES), width)
        copies.append(pltpu.make_async_copy(piece, whole.at[:, columns], sems.at[k]))
    for copy in copies:
        copy.start()
    return copies


def grad_kernel(members, cores, rows, me, stretch, shift, info, text, weights, *refs):
    images, (out, img, wt, slopes, img_sems, wt_sems) = refs[:members], refs[members:]
    chunk = wt.shape[0] // wt_sems.shape[0]
    wt_copies = []
    for k in range(wt_sems.shape[0]):
        span = slice(k * chunk, (k + 1) * chunk)
        wt_copies.append(pltpu.make_async_copy(weights.at[span], wt.at[span], wt_sems.at[k]))
        wt_copies[k].start()
    img_copies = load_columns(me[0], cores, images, img, img_sems)
    gain, offset = stretch[0], shift[0]
    pairs = text.shape[0]
    own_labels = info[me[0], 2:3, :]
    same_micro = (iota((pairs, pairs), 0) >= rows) == (iota((pairs, pairs), 1) >= rows)
    raw = jnp.zeros((pairs, wt.shape[1]), F32)
    for k, copy in enumerate(wt_copies):
        copy.wait()
        span = slice(k * chunk, (k + 1) * chunk)
        raw = raw + dot(text[:, span], wt[span, :], 1, 0)
    inverse = lax.rsqrt(jnp.sum(raw * raw, axis=1, keepdims=True) + EPS)
    unit = raw * inverse
    unit_bf = unit.astype(BF)
    for copy in img_copies:
        copy.wait()
    for g in range(members):
        span = slice(g * pairs, (g + 1) * pairs)
        block = img[span, :]
        wide = block.astype(F32)
        inv = lax.rsqrt(jnp.sum(wide * wide, axis=1, keepdims=True) + EPS)
        logit = gain * inv * dot(block, unit_bf, 1, 1) + offset
        match = (as_column(info[g, 2:3, :]) == own_labels).astype(F32)
        slope = LOSS_SCALE * inv * (jax.nn.sigmoid(logit) - match)
        slopes[span, :] = jnp.where(same_micro, slope, 0.0).astype(BF)
    grad = gain * dot(slopes[...], img[...], 0, 0)
    grad = grad - unit * jnp.sum(unit * grad, axis=1, keepdims=True)
    grad = (inverse * grad).astype(BF)
    out[...] = dot(grad, wt[...], 1, 1).astype(BF)


def make_local(nz, ny, nx, nc):
    members, owners = nx * nc, nz * ny

    def swap(v):
        return lax.ppermute(v, "core", [(i, nc - 1 - i) for i in range(nc)])

    def shift(v, by):
        return lax.ppermute(v, "x", [(i, (i + by) % nx) for i in range(nx)])

    def turn(v):
        moves = [(i * nc + c, (i + 1 - 2 * c) % nx * nc + c) for i in range(nx) for c in range(nc)]
        return lax.ppermute(v, ("x", "core"), moves)

    def whole_group(v, core):
        up, down = shift(v, 1), shift(v, -1)
        twin = swap(v)
        up, down, twin = lax.optimization_barrier((up, down, twin))
        far = turn(jnp.where(core == 0, up, down))
        return [v, up, far, down, twin, swap(up), swap(far), swap(down)]

    def local(text, cache, owner, entry, labels, wi, wt, stretch, offset):
        micro, rows, d_txt = text.shape
        d_img, emb = cache.shape[1], wi.shape[1]
        wi_rows, wt_rows = wi.shape[0], wt.shape[0]
        width = emb // members
        pairs = micro * rows
        slots = members * micro * CAP
        x, core = lax.axis_index("x"), lax.axis_index("core")
        me = x * nc + core

        wt_all = lax.all_gather(wt, ("z", "y"), axis=0, tiled=True)

        info = pl.pallas_call(
            pack_kernel,
            out_shape=jax.ShapeDtypeStruct((members, 3, pairs), I32),
            in_specs=[VMEM, VMEM, VMEM],
            out_specs=VMEM,
            compiler_params=LARGE,
        )(owner.transpose(0, 2, 1), entry, labels)
        info = lax.all_to_all(info, ("x", "core"), split_axis=0, concat_axis=0, tiled=True)
        ask, slot = pl.pallas_call(
            functools.partial(ask_kernel, micro, rows, owners),
            out_shape=(
                jax.ShapeDtypeStruct((owners, LANES), BF),
                jax.ShapeDtypeStruct((members, pairs), I32),
            ),
            in_specs=[VMEM],
            out_specs=(VMEM, VMEM),
            compiler_params=SMALL,
        )(info)

        wi_pad = -(-(wi_rows + 1) // 8) * 8
        wi_part = lax.dynamic_slice(wi, (0, me * width), (wi_rows, width))
        sent = jnp.concatenate(
            [
                jnp.broadcast_to(wi_part[None], (owners,) + wi_part.shape),
                ask[:, None, :],
                jnp.zeros((owners, wi_pad - wi_rows - 1, width), BF),
            ],
            axis=1,
        )
        got = lax.all_to_all(sent, ("z", "y"), split_axis=0, concat_axis=0, tiled=True)

        old, new = iota((d_img, owners * wi_pad), 0), iota((d_img, owners * wi_pad), 1)
        spread = (old // wi_rows * wi_pad + old % wi_rows == new).astype(BF)
        cache_pad = dot(cache, spread, 1, 0).astype(BF)
        wi_all = got.reshape(owners * wi_pad, width)
        table = dot(cache_pad, wi_all, 1, 0).astype(BF)
        asked = got[:, wi_rows, :slots].astype(I32).reshape(-1)
        pick = (asked[:, None] == jnp.arange(cache.shape[0], dtype=I32)).astype(BF)
        served = dot(pick, table, 1, 0).astype(BF).reshape(owners, slots, width)
        fetched = lax.all_to_all(served, ("z", "y"), split_axis=0, concat_axis=0, tiled=True)
        mine = pl.pallas_call(
            unsort_kernel,
            out_shape=jax.ShapeDtypeStruct((members * pairs, width), BF),
            in_specs=[VMEM, VMEM],
            out_specs=VMEM,
            compiler_params=SMALL,
        )(slot, fetched.reshape(owners * slots, width))

        image_pieces = whole_group(mine, core)
        out = pl.pallas_call(
            functools.partial(grad_kernel, members, nc, rows),
            out_shape=jax.ShapeDtypeStruct((pairs, d_txt), BF),
            in_specs=[SMEM, SMEM, SMEM, VMEM, VMEM] + [ANY] * (members + 1),
            out_specs=VMEM,
            scratch_shapes=[
                pltpu.VMEM((members * pairs, emb), BF),
                pltpu.VMEM((d_txt, emb), BF),
                pltpu.VMEM((members * pairs, pairs), BF),
                pltpu.SemaphoreType.DMA((members,)),
                pltpu.SemaphoreType.DMA((4,)),
            ],
            compiler_params=LARGE,
            cost_estimate=pl.CostEstimate(
                flops=4 * pairs * d_txt * emb, bytes_accessed=2 * d_txt * emb, transcendentals=0
            ),
        )(me.reshape(1), stretch, offset, info, text.reshape(pairs, d_txt), wt_all, *image_pieces)
        return out.reshape(micro, rows, d_txt)

    return local


def solution(mesh):
    nz, ny, nx, nc = 8, 8, 4, 2
    fine = Mesh(mesh.devices.reshape(nz, ny, nx, nc), ("z", "y", "x", "core"))
    dp, every = ("z", "y"), ("z", "y", "x", "core")
    return jax.shard_map(
        make_local(nz, ny, nx, nc),
        mesh=fine,
        in_specs=(
            P(None, every, None),
            P(dp, None),
            P(None, every, None),
            P(None, every),
            P(None, every),
            P(dp, None),
            P(dp, None),
            P(),
            P(),
        ),
        out_specs=P(None, every, None),
        check_vma=False,
    )
```

```python
import functools

import jax
import jax.numpy as jnp
from jax import lax
from jax.experimental import pallas as pl
from jax.experimental.pallas import tpu as pltpu
from jax.sharding import Mesh, PartitionSpec as P

EPS = 1e-06
LOSS_SCALE = 256.0
CAP = 2
HOPS = (0, 2, 3, 1)
LANES = 128
BF = jnp.bfloat16
F32 = jnp.float32
I32 = jnp.int32
VMEM = pl.BlockSpec(memory_space=pltpu.VMEM)
SMEM = pl.BlockSpec(memory_space=pltpu.SMEM)
ANY = pl.BlockSpec(memory_space=pl.ANY)
SMALL = pltpu.CompilerParams(vmem_limit_bytes=16 * 1024 * 1024)
LARGE = pltpu.CompilerParams(vmem_limit_bytes=58 * 1024 * 1024)


def dot(a, b, left, right):
    return lax.dot_general(a, b, (((left,), (right,)), ((), ())), preferred_element_type=F32)


def iota(shape, dim):
    return lax.broadcasted_iota(I32, shape, dim)


def as_column(row):
    return jnp.broadcast_to(row, (row.shape[1], row.shape[1])).T


def pack_kernel(owner, entry, labels, info):
    micro = owner.shape[0]
    lines = [
        [owner[m] for m in range(micro)],
        [entry[m:m + 1, :] for m in range(micro)],
        [labels[m:m + 1, :] for m in range(micro)],
    ]
    for k, line in enumerate(lines):
        line = jnp.concatenate(line, axis=1)
        for g in range(info.shape[0]):
            info[g, k:k + 1, :] = line


def ask_kernel(micro, rows, owners, info, ask, slot):
    members = info.shape[0]
    pairs, slots = micro * rows, members * micro * CAP
    r, c = iota((pairs, pairs), 0), iota((pairs, pairs), 1)
    before = ((r < c) & ((r >= rows) == (c >= rows))).astype(F32).astype(BF)
    owner_id, slot_id = iota((owners, pairs), 0), iota((LANES, pairs), 0)
    half = (iota((1, pairs), 1) >= rows).astype(I32) * CAP
    total = jnp.zeros((owners, LANES), F32)
    for g in range(members):
        own, pos = info[g, 0:1, :], info[g, 1:2, :]
        hit = own == owner_id
        hits = hit.astype(F32)
        earlier = dot(hits.astype(BF), before, 1, 0)
        nth = jnp.sum(hits * earlier, axis=0, keepdims=True).astype(I32)
        place = g * micro * CAP + half + nth
        slot[g:g + 1, :] = own * slots + place
        put = jnp.where(place == slot_id, pos, 0).astype(F32).astype(BF)
        total = total + dot(hits.astype(BF), put, 1, 1)
    ask[...] = total.astype(BF)


def unsort_kernel(slot, fetched, mine):
    members, pairs = slot.shape
    count = fetched.shape[0]
    lane = iota((pairs, count), 1)
    for g in range(members):
        column = as_column(slot[g:g + 1, :])
        where = (lane == jnp.concatenate([column] * (count // pairs), axis=1)).astype(F32).astype(BF)
        mine[g * pairs:(g + 1) * pairs, :] = dot(where, fetched[...], 1, 0).astype(BF)


def load_columns(me, cores, pieces, whole, sems):
    chips, width = len(pieces) // cores, whole.shape[1] // len(pieces)
    x, core = me // cores, me % cores
    copies = []
    for k, piece in enumerate(pieces):
        member = (x + chips - HOPS[k % chips]) % chips * cores + (core ^ (k // chips))
        columns = pl.ds(pl.multiple_of(member * width, LANES), width)
        copies.append(pltpu.make_async_copy(piece, whole.at[:, columns], sems.at[k]))
    for copy in copies:
        copy.start()
    return copies


def grad_kernel(members, cores, rows, me, stretch, shift, info, text, weights, *refs):
    images, (out, img, wt, norms, matches, slopes, img_sems, wt_sems) = refs[:members], refs[members:]
    img_copies = load_columns(me[0], cores, images, img, img_sems)
    chunk = wt.shape[0] // wt_sems.shape[0]
    wt_copies = []
    for k in range(wt_sems.shape[0]):
        span = slice(k * chunk, (k + 1) * chunk)
        wt_copies.append(pltpu.make_async_copy(weights.at[span], wt.at[span], wt_sems.at[k]))
        wt_copies[k].start()
    gain, offset = stretch[0], shift[0]
    pairs = text.shape[0]
    own_labels = info[me[0], 2:3, :]
    for g in range(members):
        span = slice(g * pairs, (g + 1) * pairs)
        matches[span, :] = (as_column(info[g, 2:3, :]) == own_labels).astype(F32)
    for copy in img_copies:
        copy.wait()
    for g in range(members):
        span = slice(g * pairs, (g + 1) * pairs)
        wide = img[span, :].astype(F32)
        inv = lax.rsqrt(jnp.sum(wide * wide, axis=1, keepdims=True) + EPS)
        norms[span, :] = jnp.broadcast_to(inv, (pairs, pairs))
    raw = jnp.zeros((pairs, wt.shape[1]), F32)
    for k, copy in enumerate(wt_copies):
        copy.wait()
        span = slice(k * chunk, (k + 1) * chunk)
        raw = raw + dot(text[:, span], wt[span, :], 1, 0)
    inverse = lax.rsqrt(jnp.sum(raw * raw, axis=1, keepdims=True) + EPS)
    unit = raw * inverse
    similar = dot(img[...], unit.astype(BF), 1, 1)
    same_micro = (iota((pairs, pairs), 0) >= rows) == (iota((pairs, pairs), 1) >= rows)
    for g in range(members):
        span = slice(g * pairs, (g + 1) * pairs)
        inv = norms[span, :]
        logit = gain * inv * similar[span, :] + offset
        slope = LOSS_SCALE * inv * (jax.nn.sigmoid(logit) - matches[span, :])
        slopes[span, :] = jnp.where(same_micro, slope, 0.0).astype(BF)
    grad = gain * dot(slopes[...], img[...], 0, 0)
    grad = grad - unit * jnp.sum(unit * grad, axis=1, keepdims=True)
    grad = (inverse * grad).astype(BF)
    out[...] = dot(grad, wt[...], 1, 1).astype(BF)


def make_local(nz, ny, nx, nc):
    members, owners = nx * nc, nz * ny

    def swap(v):
        return lax.ppermute(v, "core", [(i, nc - 1 - i) for i in range(nc)])

    def shift(v, by):
        return lax.ppermute(v, "x", [(i, (i + by) % nx) for i in range(nx)])

    def whole_group(v):
        near = [v] + [shift(v, hop) for hop in HOPS[1:]]
        return near + [swap(p) for p in near]

    def local(text, cache, owner, entry, labels, wi, wt, stretch, offset):
        micro, rows, d_txt = text.shape
        d_img, emb = cache.shape[1], wi.shape[1]
        wi_rows, wt_rows = wi.shape[0], wt.shape[0]
        width = emb // members
        pairs = micro * rows
        slots = members * micro * CAP
        x, core = lax.axis_index("x"), lax.axis_index("core")
        me = x * nc + core

        wt_all = lax.all_gather(wt, ("z", "y"), axis=0, tiled=True)

        info = pl.pallas_call(
            pack_kernel,
            out_shape=jax.ShapeDtypeStruct((members, 3, pairs), I32),
            in_specs=[VMEM, VMEM, VMEM],
            out_specs=VMEM,
            compiler_params=LARGE,
        )(owner.transpose(0, 2, 1), entry, labels)
        info = lax.all_to_all(info, ("x", "core"), split_axis=0, concat_axis=0, tiled=True)
        ask, slot = pl.pallas_call(
            functools.partial(ask_kernel, micro, rows, owners),
            out_shape=(
                jax.ShapeDtypeStruct((owners, LANES), BF),
                jax.ShapeDtypeStruct((members, pairs), I32),
            ),
            in_specs=[VMEM],
            out_specs=(VMEM, VMEM),
            compiler_params=SMALL,
        )(info)

        wi_pad = -(-(wi_rows + 1) // 8) * 8
        wi_part = lax.dynamic_slice(wi, (0, me * width), (wi_rows, width))
        sent = jnp.concatenate(
            [
                jnp.broadcast_to(wi_part[None], (owners,) + wi_part.shape),
                ask[:, None, :],
                jnp.zeros((owners, wi_pad - wi_rows - 1, width), BF),
            ],
            axis=1,
        )
        got = lax.all_to_all(sent, ("z", "y"), split_axis=0, concat_axis=0, tiled=True)

        old, new = iota((d_img, owners * wi_pad), 0), iota((d_img, owners * wi_pad), 1)
        spread = (old // wi_rows * wi_pad + old % wi_rows == new).astype(BF)
        cache_pad = dot(cache, spread, 1, 0).astype(BF)
        wi_all = got.reshape(owners * wi_pad, width)
        table = dot(cache_pad, wi_all, 1, 0).astype(BF)
        asked = got[:, wi_rows, :slots].astype(I32).reshape(-1)
        pick = (asked[:, None] == jnp.arange(cache.shape[0], dtype=I32)).astype(BF)
        served = dot(pick, table, 1, 0).astype(BF).reshape(owners, slots, width)
        fetched = lax.all_to_all(served, ("z", "y"), split_axis=0, concat_axis=0, tiled=True)
        mine = pl.pallas_call(
            unsort_kernel,
            out_shape=jax.ShapeDtypeStruct((members * pairs, width), BF),
            in_specs=[VMEM, VMEM],
            out_specs=VMEM,
            compiler_params=SMALL,
        )(slot, fetched.reshape(owners * slots, width))

        image_pieces = whole_group(mine)
        out = pl.pallas_call(
            functools.partial(grad_kernel, members, nc, rows),
            out_shape=jax.ShapeDtypeStruct((pairs, d_txt), BF),
            in_specs=[SMEM, SMEM, SMEM, VMEM, VMEM] + [ANY] * (members + 1),
            out_specs=VMEM,
            scratch_shapes=[
                pltpu.VMEM((members * pairs, emb), BF),
                pltpu.VMEM((d_txt, emb), BF),
                pltpu.VMEM((members * pairs, pairs), F32),
                pltpu.VMEM((members * pairs, pairs), F32),
                pltpu.VMEM((members * pairs, pairs), BF),
                pltpu.SemaphoreType.DMA((members,)),
                pltpu.SemaphoreType.DMA((4,)),
            ],
            compiler_params=LARGE,
            cost_estimate=pl.CostEstimate(
                flops=4 * pairs * d_txt * emb, bytes_accessed=2 * d_txt * emb, transcendentals=0
            ),
        )(me.reshape(1), stretch, offset, info, text.reshape(pairs, d_txt), wt_all, *image_pieces)
        return out.reshape(micro, rows, d_txt)

    return local


def solution(mesh):
    nz, ny, nx, nc = 8, 8, 4, 2
    fine = Mesh(mesh.devices.reshape(nz, ny, nx, nc), ("z", "y", "x", "core"))
    dp, every = ("z", "y"), ("z", "y", "x", "core")
    return jax.shard_map(
        make_local(nz, ny, nx, nc),
        mesh=fine,
        in_specs=(
            P(None, every, None),
            P(dp, None),
            P(None, every, None),
            P(None, every),
            P(None, every),
            P(dp, None),
            P(dp, None),
            P(),
            P(),
        ),
        out_specs=P(None, every, None),
        check_vma=False,
    )
```

```python
import functools

import jax
import jax.numpy as jnp
from jax import lax
from jax.experimental import pallas as pl
from jax.experimental.pallas import tpu as pltpu
from jax.sharding import Mesh, PartitionSpec as P

EPS = 1e-06
LOSS_SCALE = 256.0
CAP = 2
HOPS = (0, 1, 3, 2)
LANES = 128
BF = jnp.bfloat16
F32 = jnp.float32
I32 = jnp.int32
VMEM = pl.BlockSpec(memory_space=pltpu.VMEM)
SMEM = pl.BlockSpec(memory_space=pltpu.SMEM)
ANY = pl.BlockSpec(memory_space=pl.ANY)
SMALL = pltpu.CompilerParams(vmem_limit_bytes=16 * 1024 * 1024)
LARGE = pltpu.CompilerParams(vmem_limit_bytes=58 * 1024 * 1024)


def dot(a, b, left, right):
    return lax.dot_general(a, b, (((left,), (right,)), ((), ())), preferred_element_type=F32)


def iota(shape, dim):
    return lax.broadcasted_iota(I32, shape, dim)


def as_column(row):
    return jnp.broadcast_to(row, (row.shape[1], row.shape[1])).T


def pack_kernel(owner, entry, labels, info):
    micro = owner.shape[0]
    lines = [
        [owner[m] for m in range(micro)],
        [entry[m:m + 1, :] for m in range(micro)],
        [labels[m:m + 1, :] for m in range(micro)],
    ]
    for k, line in enumerate(lines):
        line = jnp.concatenate(line, axis=1)
        for g in range(info.shape[0]):
            info[g, k:k + 1, :] = line


def ask_kernel(micro, rows, owners, info, ask, slot):
    members = info.shape[0]
    pairs, slots = micro * rows, members * micro * CAP
    r, c = iota((pairs, pairs), 0), iota((pairs, pairs), 1)
    before = ((r < c) & ((r >= rows) == (c >= rows))).astype(F32).astype(BF)
    owner_id, slot_id = iota((owners, pairs), 0), iota((LANES, pairs), 0)
    half = (iota((1, pairs), 1) >= rows).astype(I32) * CAP
    total = jnp.zeros((owners, LANES), F32)
    for g in range(members):
        own, pos = info[g, 0:1, :], info[g, 1:2, :]
        hit = own == owner_id
        hits = hit.astype(F32)
        earlier = dot(hits.astype(BF), before, 1, 0)
        nth = jnp.sum(hits * earlier, axis=0, keepdims=True).astype(I32)
        place = g * micro * CAP + half + nth
        slot[g:g + 1, :] = own * slots + place
        put = jnp.where(place == slot_id, pos, 0).astype(F32).astype(BF)
        total = total + dot(hits.astype(BF), put, 1, 1)
    ask[...] = total.astype(BF)


def unsort_kernel(slot, fetched, mine):
    members, pairs = slot.shape
    count = fetched.shape[0]
    lane = iota((pairs, count), 1)
    for g in range(members):
        column = as_column(slot[g:g + 1, :])
        where = (lane == jnp.concatenate([column] * (count // pairs), axis=1)).astype(F32).astype(BF)
        mine[g * pairs:(g + 1) * pairs, :] = dot(where, fetched[...], 1, 0).astype(BF)


def load_columns(me, cores, pieces, whole, sems):
    chips, width = len(pieces) // cores, whole.shape[1] // len(pieces)
    x, core = me // cores, me % cores
    copies = []
    for k, piece in enumerate(pieces):
        member = (x + chips - HOPS[k % chips]) % chips * cores + (core ^ (k // chips))
        columns = pl.ds(pl.multiple_of(member * width, LANES), width)
        copies.append(pltpu.make_async_copy(piece, whole.at[:, columns], sems.at[k]))
    for copy in copies:
        copy.start()
    return copies


def image_kernel(members, cores, me, info, *refs):
    images, (whole, norms, matches, img, sems, out_sem) = refs[:members], refs[members:]
    copies = load_columns(me[0], cores, images, img, sems)
    pairs = matches.shape[1]
    own_labels = info[me[0], 2:3, :]
    for g in range(members):
        span = slice(g * pairs, (g + 1) * pairs)
        matches[span, :] = (as_column(info[g, 2:3, :]) == own_labels).astype(F32)
    for copy in copies:
        copy.wait()
    write = pltpu.make_async_copy(img, whole, out_sem)
    write.start()
    for g in range(members):
        span = slice(g * pairs, (g + 1) * pairs)
        wide = img[span, :].astype(F32)
        inv = lax.rsqrt(jnp.sum(wide * wide, axis=1, keepdims=True) + EPS)
        norms[span, :] = jnp.broadcast_to(inv, (pairs, pairs))
    write.wait()


def grad_kernel(rows, stretch, shift, text_in, weights, img_in, norms_in, matches_in, out,
                text, wt, img, norms, matches, slopes, wt_sems, sems):
    ins, bufs = (text_in, img_in, norms_in, matches_in), (text, img, norms, matches)
    copies = [pltpu.make_async_copy(a, b, sems.at[k]) for k, (a, b) in enumerate(zip(ins, bufs))]
    chunk = wt.shape[0] // wt_sems.shape[0]
    spans = [slice(k * chunk, (k + 1) * chunk) for k in range(wt_sems.shape[0])]
    wt_copies = [pltpu.make_async_copy(weights.at[p], wt.at[p], wt_sems.at[k]) for k, p in enumerate(spans)]
    for copy in copies[:1] + wt_copies + copies[1:]:
        copy.start()
    gain, offset = stretch[0], shift[0]
    pairs = text.shape[0]
    same_micro = (iota((pairs, pairs), 0) >= rows) == (iota((pairs, pairs), 1) >= rows)
    copies[0].wait()
    raw = jnp.zeros((pairs, wt.shape[1]), F32)
    for copy, span in zip(wt_copies, spans):
        copy.wait()
        raw = raw + dot(text[:, span], wt[span, :], 1, 0)
    inverse = lax.rsqrt(jnp.sum(raw * raw, axis=1, keepdims=True) + EPS)
    unit = raw * inverse
    for copy in copies[1:]:
        copy.wait()
    similar = dot(img[...], unit.astype(BF), 1, 1)
    for g in range(img.shape[0] // pairs):
        span = slice(g * pairs, (g + 1) * pairs)
        inv = norms[span, :]
        logit = gain * inv * similar[span, :] + offset
        slope = LOSS_SCALE * inv * (jax.nn.sigmoid(logit) - matches[span, :])
        slopes[span, :] = jnp.where(same_micro, slope, 0.0).astype(BF)
    grad = gain * dot(slopes[...], img[...], 0, 0)
    grad = grad - unit * jnp.sum(unit * grad, axis=1, keepdims=True)
    grad = (inverse * grad).astype(BF)
    out[...] = dot(grad, wt[...], 1, 1).astype(BF)


def make_local(nz, ny, nx, nc):
    members, owners = nx * nc, nz * ny

    def swap(v):
        return lax.ppermute(v, "core", [(i, nc - 1 - i) for i in range(nc)])

    def shift(v, by):
        return lax.ppermute(v, "x", [(i, (i + by) % nx) for i in range(nx)])

    def whole_group(v):
        near = [v] + [shift(v, hop) for hop in HOPS[1:]]
        return near + [swap(p) for p in near]

    def local(text, cache, owner, entry, labels, wi, wt, stretch, offset):
        micro, rows, d_txt = text.shape
        d_img, emb = cache.shape[1], wi.shape[1]
        wi_rows, wt_rows = wi.shape[0], wt.shape[0]
        width = emb // members
        pairs = micro * rows
        slots = members * micro * CAP
        x, core = lax.axis_index("x"), lax.axis_index("core")
        me = x * nc + core

        wt_all = lax.all_gather(wt, ("z", "y"), axis=0, tiled=True)

        info = pl.pallas_call(
            pack_kernel,
            out_shape=jax.ShapeDtypeStruct((members, 3, pairs), I32),
            in_specs=[VMEM, VMEM, VMEM],
            out_specs=VMEM,
            compiler_params=LARGE,
        )(owner.transpose(0, 2, 1), entry, labels)
        info = lax.all_to_all(info, ("x", "core"), split_axis=0, concat_axis=0, tiled=True)
        ask, slot = pl.pallas_call(
            functools.partial(ask_kernel, micro, rows, owners),
            out_shape=(
                jax.ShapeDtypeStruct((owners, LANES), BF),
                jax.ShapeDtypeStruct((members, pairs), I32),
            ),
            in_specs=[VMEM],
            out_specs=(VMEM, VMEM),
            compiler_params=SMALL,
        )(info)

        wi_pad = -(-(wi_rows + 1) // 8) * 8
        wi_part = lax.dynamic_slice(wi, (0, me * width), (wi_rows, width))
        sent = jnp.concatenate(
            [
                jnp.broadcast_to(wi_part[None], (owners,) + wi_part.shape),
                ask[:, None, :],
                jnp.zeros((owners, wi_pad - wi_rows - 1, width), BF),
            ],
            axis=1,
        )
        got = lax.all_to_all(sent, ("z", "y"), split_axis=0, concat_axis=0, tiled=True)

        old, new = iota((d_img, owners * wi_pad), 0), iota((d_img, owners * wi_pad), 1)
        spread = (old // wi_rows * wi_pad + old % wi_rows == new).astype(BF)
        cache_pad = dot(cache, spread, 1, 0).astype(BF)
        wi_all = got.reshape(owners * wi_pad, width)
        table = dot(cache_pad, wi_all, 1, 0).astype(BF)
        asked = got[:, wi_rows, :slots].astype(I32).reshape(-1)
        pick = (asked[:, None] == jnp.arange(cache.shape[0], dtype=I32)).astype(BF)
        served = dot(pick, table, 1, 0).astype(BF).reshape(owners, slots, width)
        fetched = lax.all_to_all(served, ("z", "y"), split_axis=0, concat_axis=0, tiled=True)
        mine = pl.pallas_call(
            unsort_kernel,
            out_shape=jax.ShapeDtypeStruct((members * pairs, width), BF),
            in_specs=[VMEM, VMEM],
            out_specs=VMEM,
            compiler_params=SMALL,
        )(slot, fetched.reshape(owners * slots, width))

        image_pieces = whole_group(mine)
        images = members * pairs
        img, norms, matches = pl.pallas_call(
            functools.partial(image_kernel, members, nc),
            out_shape=(
                jax.ShapeDtypeStruct((images, emb), BF),
                jax.ShapeDtypeStruct((images, pairs), F32),
                jax.ShapeDtypeStruct((images, pairs), F32),
            ),
            in_specs=[SMEM, VMEM] + [ANY] * members,
            out_specs=(ANY, VMEM, VMEM),
            scratch_shapes=[
                pltpu.VMEM((images, emb), BF),
                pltpu.SemaphoreType.DMA((members,)),
                pltpu.SemaphoreType.DMA,
            ],
            compiler_params=SMALL,
        )(me.reshape(1), info, *image_pieces)
        out = pl.pallas_call(
            functools.partial(grad_kernel, rows),
            out_shape=jax.ShapeDtypeStruct((pairs, d_txt), BF),
            in_specs=[SMEM, SMEM] + [ANY] * 5,
            out_specs=VMEM,
            scratch_shapes=[
                pltpu.VMEM((pairs, d_txt), BF),
                pltpu.VMEM((d_txt, emb), BF),
                pltpu.VMEM((images, emb), BF),
                pltpu.VMEM((images, pairs), F32),
                pltpu.VMEM((images, pairs), F32),
                pltpu.VMEM((images, pairs), BF),
                pltpu.SemaphoreType.DMA((4,)),
                pltpu.SemaphoreType.DMA((4,)),
            ],
            compiler_params=LARGE,
            cost_estimate=pl.CostEstimate(
                flops=4 * pairs * d_txt * emb, bytes_accessed=2 * d_txt * emb, transcendentals=0
            ),
        )(stretch, offset, text.reshape(pairs, d_txt), wt_all, img, norms, matches)
        return out.reshape(micro, rows, d_txt)

    return local


def solution(mesh):
    nz, ny, nx, nc = 8, 8, 4, 2
    fine = Mesh(mesh.devices.reshape(nz, ny, nx, nc), ("z", "y", "x", "core"))
    dp, every = ("z", "y"), ("z", "y", "x", "core")
    return jax.shard_map(
        make_local(nz, ny, nx, nc),
        mesh=fine,
        in_specs=(
            P(None, every, None),
            P(dp, None),
            P(None, every, None),
            P(None, every),
            P(None, every),
            P(dp, None),
            P(dp, None),
            P(),
            P(),
        ),
        out_specs=P(None, every, None),
        check_vma=False,
    )
```

```python
import functools

import jax
import jax.numpy as jnp
from jax import lax
from jax.experimental import pallas as pl
from jax.experimental.pallas import tpu as pltpu
from jax.sharding import Mesh, PartitionSpec as P

EPS = 1e-06
LOSS_SCALE = 256.0
CAP = 2
HOPS = (0, 1, 3, 2)
LANES = 128
BF = jnp.bfloat16
F32 = jnp.float32
I32 = jnp.int32
VMEM = pl.BlockSpec(memory_space=pltpu.VMEM)
SMEM = pl.BlockSpec(memory_space=pltpu.SMEM)
ANY = pl.BlockSpec(memory_space=pl.ANY)
SMALL = pltpu.CompilerParams(vmem_limit_bytes=16 * 1024 * 1024)
LARGE = pltpu.CompilerParams(vmem_limit_bytes=58 * 1024 * 1024)


def dot(a, b, left, right):
    return lax.dot_general(a, b, (((left,), (right,)), ((), ())), preferred_element_type=F32)


def iota(shape, dim):
    return lax.broadcasted_iota(I32, shape, dim)


def as_column(row):
    return jnp.broadcast_to(row, (row.shape[1], row.shape[1])).T


def pack_kernel(owner, entry, labels, info):
    micro = owner.shape[0]
    lines = [
        [owner[m] for m in range(micro)],
        [entry[m:m + 1, :] for m in range(micro)],
        [labels[m:m + 1, :] for m in range(micro)],
    ]
    for k, line in enumerate(lines):
        line = jnp.concatenate(line, axis=1)
        for g in range(info.shape[0]):
            info[g, k:k + 1, :] = line


def ask_kernel(micro, rows, owners, info, ask, slot):
    members = info.shape[0]
    pairs, slots = micro * rows, members * micro * CAP
    r, c = iota((pairs, pairs), 0), iota((pairs, pairs), 1)
    before = ((r < c) & ((r >= rows) == (c >= rows))).astype(F32).astype(BF)
    owner_id, slot_id = iota((owners, pairs), 0), iota((LANES, pairs), 0)
    half = (iota((1, pairs), 1) >= rows).astype(I32) * CAP
    total = jnp.zeros((owners, LANES), F32)
    for g in range(members):
        own, pos = info[g, 0:1, :], info[g, 1:2, :]
        hit = own == owner_id
        hits = hit.astype(F32)
        earlier = dot(hits.astype(BF), before, 1, 0)
        nth = jnp.sum(hits * earlier, axis=0, keepdims=True).astype(I32)
        place = g * micro * CAP + half + nth
        slot[g:g + 1, :] = own * slots + place
        put = jnp.where(place == slot_id, pos, 0).astype(F32).astype(BF)
        total = total + dot(hits.astype(BF), put, 1, 1)
    ask[...] = total.astype(BF)


def unsort_kernel(slot, fetched, mine):
    members, pairs = slot.shape
    count = fetched.shape[0]
    lane = iota((pairs, count), 1)
    for g in range(members):
        column = as_column(slot[g:g + 1, :])
        where = (lane == jnp.concatenate([column] * (count // pairs), axis=1)).astype(F32).astype(BF)
        mine[g * pairs:(g + 1) * pairs, :] = dot(where, fetched[...], 1, 0).astype(BF)


def load_columns(me, cores, pieces, whole, sems):
    chips, width = len(pieces) // cores, whole.shape[1] // len(pieces)
    x, core = me // cores, me % cores
    copies = []
    for k, piece in enumerate(pieces):
        member = (x + chips - HOPS[k % chips]) % chips * cores + (core ^ (k // chips))
        columns = pl.ds(pl.multiple_of(member * width, LANES), width)
        copies.append(pltpu.make_async_copy(piece, whole.at[:, columns], sems.at[k]))
    for copy in copies:
        copy.start()
    return copies


def image_kernel(members, cores, me, info, *refs):
    images, (whole, norms, matches, img, sems, out_sem) = refs[:members], refs[members:]
    copies = load_columns(me[0], cores, images, img, sems)
    pairs = matches.shape[1]
    own_labels = info[me[0], 2:3, :]
    for g in range(members):
        span = slice(g * pairs, (g + 1) * pairs)
        matches[span, :] = (as_column(info[g, 2:3, :]) == own_labels).astype(F32)
    for copy in copies:
        copy.wait()
    write = pltpu.make_async_copy(img, whole, out_sem)
    write.start()
    for g in range(members):
        span = slice(g * pairs, (g + 1) * pairs)
        wide = img[span, :].astype(F32)
        inv = lax.rsqrt(jnp.sum(wide * wide, axis=1, keepdims=True) + EPS)
        norms[span, :] = jnp.broadcast_to(inv, (pairs, pairs))
    write.wait()


def grad_kernel(rows, stretch, shift, text_in, weights, img_in, norms_in, matches_in, out,
                text, wt, img, norms, matches, slopes, wt_sems, sems):
    ins, bufs = (text_in, img_in, norms_in, matches_in), (text, img, norms, matches)
    copies = [pltpu.make_async_copy(a, b, sems.at[k]) for k, (a, b) in enumerate(zip(ins, bufs))]
    chunk = wt.shape[0] // wt_sems.shape[0]
    spans = [slice(k * chunk, (k + 1) * chunk) for k in range(wt_sems.shape[0])]
    wt_copies = [pltpu.make_async_copy(weights.at[p], wt.at[p], wt_sems.at[k]) for k, p in enumerate(spans)]
    for copy in copies[:1] + wt_copies + copies[1:]:
        copy.start()
    gain, offset = stretch[0], shift[0]
    pairs = text.shape[0]
    same_micro = (iota((pairs, pairs), 0) >= rows) == (iota((pairs, pairs), 1) >= rows)
    copies[0].wait()
    raw = jnp.zeros((pairs, wt.shape[1]), F32)
    for copy, span in zip(wt_copies, spans):
        copy.wait()
        raw = raw + dot(text[:, span], wt[span, :], 1, 0)
    inverse = lax.rsqrt(jnp.sum(raw * raw, axis=1, keepdims=True) + EPS)
    unit = raw * inverse
    for copy in copies[1:]:
        copy.wait()
    unit_bf = unit.astype(BF)
    for g in range(img.shape[0] // pairs):
        span = slice(g * pairs, (g + 1) * pairs)
        inv = norms[span, :]
        logit = gain * inv * dot(img[span, :], unit_bf, 1, 1) + offset
        slope = LOSS_SCALE * inv * (jax.nn.sigmoid(logit) - matches[span, :])
        slopes[span, :] = jnp.where(same_micro, slope, 0.0).astype(BF)
    grad = gain * dot(slopes[...], img[...], 0, 0)
    grad = grad - unit * jnp.sum(unit * grad, axis=1, keepdims=True)
    grad = (inverse * grad).astype(BF)
    out[...] = dot(grad, wt[...], 1, 1).astype(BF)


def make_local(nz, ny, nx, nc):
    members, owners = nx * nc, nz * ny

    def swap(v):
        return lax.ppermute(v, "core", [(i, nc - 1 - i) for i in range(nc)])

    def shift(v, by):
        return lax.ppermute(v, "x", [(i, (i + by) % nx) for i in range(nx)])

    def whole_group(v):
        near = [v] + [shift(v, hop) for hop in HOPS[1:]]
        return near + [swap(p) for p in near]

    def local(text, cache, owner, entry, labels, wi, wt, stretch, offset):
        micro, rows, d_txt = text.shape
        d_img, emb = cache.shape[1], wi.shape[1]
        wi_rows, wt_rows = wi.shape[0], wt.shape[0]
        width = emb // members
        pairs = micro * rows
        slots = members * micro * CAP
        x, core = lax.axis_index("x"), lax.axis_index("core")
        me = x * nc + core

        wt_all = lax.all_gather(wt, ("z", "y"), axis=0, tiled=True)

        info = pl.pallas_call(
            pack_kernel,
            out_shape=jax.ShapeDtypeStruct((members, 3, pairs), I32),
            in_specs=[VMEM, VMEM, VMEM],
            out_specs=VMEM,
            compiler_params=LARGE,
        )(owner.transpose(0, 2, 1), entry, labels)
        info = lax.all_to_all(info, ("x", "core"), split_axis=0, concat_axis=0, tiled=True)
        ask, slot = pl.pallas_call(
            functools.partial(ask_kernel, micro, rows, owners),
            out_shape=(
                jax.ShapeDtypeStruct((owners, LANES), BF),
                jax.ShapeDtypeStruct((members, pairs), I32),
            ),
            in_specs=[VMEM],
            out_specs=(VMEM, VMEM),
            compiler_params=SMALL,
        )(info)

        wi_pad = -(-(wi_rows + 1) // 8) * 8
        wi_part = lax.dynamic_slice(wi, (0, me * width), (wi_rows, width))
        sent = jnp.concatenate(
            [
                jnp.broadcast_to(wi_part[None], (owners,) + wi_part.shape),
                ask[:, None, :],
                jnp.zeros((owners, wi_pad - wi_rows - 1, width), BF),
            ],
            axis=1,
        )
        got = lax.all_to_all(sent, ("z", "y"), split_axis=0, concat_axis=0, tiled=True)

        old, new = iota((d_img, owners * wi_pad), 0), iota((d_img, owners * wi_pad), 1)
        spread = (old // wi_rows * wi_pad + old % wi_rows == new).astype(BF)
        cache_pad = dot(cache, spread, 1, 0).astype(BF)
        wi_all = got.reshape(owners * wi_pad, width)
        table = dot(cache_pad, wi_all, 1, 0).astype(BF)
        asked = got[:, wi_rows, :slots].astype(I32).reshape(-1)
        pick = (asked[:, None] == jnp.arange(cache.shape[0], dtype=I32)).astype(BF)
        served = dot(pick, table, 1, 0).astype(BF).reshape(owners, slots, width)
        fetched = lax.all_to_all(served, ("z", "y"), split_axis=0, concat_axis=0, tiled=True)
        mine = pl.pallas_call(
            unsort_kernel,
            out_shape=jax.ShapeDtypeStruct((members * pairs, width), BF),
            in_specs=[VMEM, VMEM],
            out_specs=VMEM,
            compiler_params=SMALL,
        )(slot, fetched.reshape(owners * slots, width))

        image_pieces = whole_group(mine)
        images = members * pairs
        img, norms, matches = pl.pallas_call(
            functools.partial(image_kernel, members, nc),
            out_shape=(
                jax.ShapeDtypeStruct((images, emb), BF),
                jax.ShapeDtypeStruct((images, pairs), F32),
                jax.ShapeDtypeStruct((images, pairs), F32),
            ),
            in_specs=[SMEM, VMEM] + [ANY] * members,
            out_specs=(ANY, VMEM, VMEM),
            scratch_shapes=[
                pltpu.VMEM((images, emb), BF),
                pltpu.SemaphoreType.DMA((members,)),
                pltpu.SemaphoreType.DMA,
            ],
            compiler_params=LARGE,
        )(me.reshape(1), info, *image_pieces)
        out = pl.pallas_call(
            functools.partial(grad_kernel, rows),
            out_shape=jax.ShapeDtypeStruct((pairs, d_txt), BF),
            in_specs=[SMEM, SMEM] + [ANY] * 5,
            out_specs=VMEM,
            scratch_shapes=[
                pltpu.VMEM((pairs, d_txt), BF),
                pltpu.VMEM((d_txt, emb), BF),
                pltpu.VMEM((images, emb), BF),
                pltpu.VMEM((images, pairs), F32),
                pltpu.VMEM((images, pairs), F32),
                pltpu.VMEM((images, pairs), BF),
                pltpu.SemaphoreType.DMA((4,)),
                pltpu.SemaphoreType.DMA((4,)),
            ],
            compiler_params=LARGE,
            cost_estimate=pl.CostEstimate(
                flops=4 * pairs * d_txt * emb, bytes_accessed=2 * d_txt * emb, transcendentals=0
            ),
        )(stretch, offset, text.reshape(pairs, d_txt), wt_all, img, norms, matches)
        return out.reshape(micro, rows, d_txt)

    return local


def solution(mesh):
    nz, ny, nx, nc = 8, 8, 4, 2
    fine = Mesh(mesh.devices.reshape(nz, ny, nx, nc), ("z", "y", "x", "core"))
    dp, every = ("z", "y"), ("z", "y", "x", "core")
    return jax.shard_map(
        make_local(nz, ny, nx, nc),
        mesh=fine,
        in_specs=(
            P(None, every, None),
            P(dp, None),
            P(None, every, None),
            P(None, every),
            P(None, every),
            P(dp, None),
            P(dp, None),
            P(),
            P(),
        ),
        out_specs=P(None, every, None),
        check_vma=False,
    )
```

```python
import functools

import jax
import jax.numpy as jnp
from jax import lax
from jax.experimental import pallas as pl
from jax.experimental.pallas import tpu as pltpu
from jax.sharding import Mesh, PartitionSpec as P

EPS = 1e-06
LOSS_SCALE = 256.0
CAP = 2
HOPS = (0, 1, 3, 2)
LANES = 128
BF = jnp.bfloat16
F32 = jnp.float32
I32 = jnp.int32
VMEM = pl.BlockSpec(memory_space=pltpu.VMEM)
SMEM = pl.BlockSpec(memory_space=pltpu.SMEM)
ANY = pl.BlockSpec(memory_space=pl.ANY)
SMALL = pltpu.CompilerParams(vmem_limit_bytes=16 * 1024 * 1024)
LARGE = pltpu.CompilerParams(vmem_limit_bytes=58 * 1024 * 1024)


def dot(a, b, left, right):
    return lax.dot_general(a, b, (((left,), (right,)), ((), ())), preferred_element_type=F32)


def iota(shape, dim):
    return lax.broadcasted_iota(I32, shape, dim)


def as_column(row):
    return jnp.broadcast_to(row, (row.shape[1], row.shape[1])).T


def pack_kernel(owner, entry, labels, info):
    micro = owner.shape[0]
    lines = [
        [owner[m] for m in range(micro)],
        [entry[m:m + 1, :] for m in range(micro)],
        [labels[m:m + 1, :] for m in range(micro)],
    ]
    for k, line in enumerate(lines):
        line = jnp.concatenate(line, axis=1)
        for g in range(info.shape[0]):
            info[g, k:k + 1, :] = line


def ask_kernel(micro, rows, owners, info, ask, slot):
    members = info.shape[0]
    pairs, slots = micro * rows, members * micro * CAP
    r, c = iota((pairs, pairs), 0), iota((pairs, pairs), 1)
    before = ((r < c) & ((r >= rows) == (c >= rows))).astype(F32).astype(BF)
    owner_id, slot_id = iota((owners, pairs), 0), iota((LANES, pairs), 0)
    half = (iota((1, pairs), 1) >= rows).astype(I32) * CAP
    total = jnp.zeros((owners, LANES), F32)
    for g in range(members):
        own, pos = info[g, 0:1, :], info[g, 1:2, :]
        hit = own == owner_id
        hits = hit.astype(F32)
        earlier = dot(hits.astype(BF), before, 1, 0)
        nth = jnp.sum(hits * earlier, axis=0, keepdims=True).astype(I32)
        place = g * micro * CAP + half + nth
        slot[g:g + 1, :] = own * slots + place
        put = jnp.where(place == slot_id, pos, 0).astype(F32).astype(BF)
        total = total + dot(hits.astype(BF), put, 1, 1)
    ask[...] = total.astype(BF)


def unsort_kernel(slot, fetched, mine):
    members, pairs = slot.shape
    count = fetched.shape[0]
    lane = iota((pairs, count), 1)
    for g in range(members):
        column = as_column(slot[g:g + 1, :])
        where = (lane == jnp.concatenate([column] * (count // pairs), axis=1)).astype(F32).astype(BF)
        mine[g * pairs:(g + 1) * pairs, :] = dot(where, fetched[...], 1, 0).astype(BF)


def load_columns(me, cores, pieces, whole, sems):
    chips, width = len(pieces) // cores, whole.shape[1] // len(pieces)
    x, core = me // cores, me % cores
    copies = []
    for k, piece in enumerate(pieces):
        member = (x + chips - HOPS[k % chips]) % chips * cores + (core ^ (k // chips))
        columns = pl.ds(pl.multiple_of(member * width, LANES), width)
        copies.append(pltpu.make_async_copy(piece, whole.at[:, columns], sems.at[k]))
    for copy in copies:
        copy.start()
    return copies


def image_kernel(members, cores, me, *refs):
    images, (img, raw, sems) = refs[:members], refs[members:]
    for copy in load_columns(me[0], cores, images, raw, sems):
        copy.wait()
    for g in range(members):
        span = slice(g * LANES, (g + 1) * LANES)
        wide = raw[span, :].astype(F32)
        inv = lax.rsqrt(jnp.sum(wide * wide, axis=1, keepdims=True) + EPS)
        img[span, :] = (wide * inv).astype(BF)


def grad_kernel(rows, me, stretch, shift, info, text, wt, img, out, slopes):
    gain, offset = stretch[0], shift[0]
    pairs = text.shape[0]
    same_micro = (iota((pairs, pairs), 0) >= rows) == (iota((pairs, pairs), 1) >= rows)
    own_labels = info[me[0], 2:3, :]
    raw = dot(text[...], wt[...], 1, 0)
    inverse = lax.rsqrt(jnp.sum(raw * raw, axis=1, keepdims=True) + EPS)
    unit = raw * inverse
    unit_bf = unit.astype(BF)
    for g in range(img.shape[0] // pairs):
        span = slice(g * pairs, (g + 1) * pairs)
        match = (as_column(info[g, 2:3, :]) == own_labels).astype(F32)
        logit = gain * dot(img[span, :], unit_bf, 1, 1) + offset
        slope = LOSS_SCALE * (jax.nn.sigmoid(logit) - match)
        slopes[span, :] = jnp.where(same_micro, slope, 0.0).astype(BF)
    grad = gain * dot(slopes[...], img[...], 0, 0)
    grad = grad - unit * jnp.sum(unit * grad, axis=1, keepdims=True)
    grad = (inverse * grad).astype(BF)
    out[...] = dot(grad, wt[...], 1, 1).astype(BF)


def make_local(nz, ny, nx, nc):
    members, owners = nx * nc, nz * ny

    def swap(v):
        return lax.ppermute(v, "core", [(i, nc - 1 - i) for i in range(nc)])

    def shift(v, by):
        return lax.ppermute(v, "x", [(i, (i + by) % nx) for i in range(nx)])

    def whole_group(v):
        near = [v] + [shift(v, hop) for hop in HOPS[1:]]
        return near + [swap(p) for p in near]

    def local(text, cache, owner, entry, labels, wi, wt, stretch, offset):
        micro, rows, d_txt = text.shape
        d_img, emb = cache.shape[1], wi.shape[1]
        wi_rows, wt_rows = wi.shape[0], wt.shape[0]
        width = emb // members
        pairs = micro * rows
        slots = members * micro * CAP
        x, core = lax.axis_index("x"), lax.axis_index("core")
        me = x * nc + core

        wt_all = lax.all_gather(wt, ("z", "y"), axis=0, tiled=True)

        info = pl.pallas_call(
            pack_kernel,
            out_shape=jax.ShapeDtypeStruct((members, 3, pairs), I32),
            in_specs=[VMEM, VMEM, VMEM],
            out_specs=VMEM,
            compiler_params=LARGE,
        )(owner.transpose(0, 2, 1), entry, labels)
        info = lax.all_to_all(info, ("x", "core"), split_axis=0, concat_axis=0, tiled=True)
        ask, slot = pl.pallas_call(
            functools.partial(ask_kernel, micro, rows, owners),
            out_shape=(
                jax.ShapeDtypeStruct((owners, LANES), BF),
                jax.ShapeDtypeStruct((members, pairs), I32),
            ),
            in_specs=[VMEM],
            out_specs=(VMEM, VMEM),
            compiler_params=SMALL,
        )(info)

        wi_pad = -(-(wi_rows + 1) // 8) * 8
        wi_part = lax.dynamic_slice(wi, (0, me * width), (wi_rows, width))
        sent = jnp.concatenate(
            [
                jnp.broadcast_to(wi_part[None], (owners,) + wi_part.shape),
                ask[:, None, :],
                jnp.zeros((owners, wi_pad - wi_rows - 1, width), BF),
            ],
            axis=1,
        )
        got = lax.all_to_all(sent, ("z", "y"), split_axis=0, concat_axis=0, tiled=True)

        old, new = iota((d_img, owners * wi_pad), 0), iota((d_img, owners * wi_pad), 1)
        spread = (old // wi_rows * wi_pad + old % wi_rows == new).astype(BF)
        cache_pad = dot(cache, spread, 1, 0).astype(BF)
        wi_all = got.reshape(owners * wi_pad, width)
        table = dot(cache_pad, wi_all, 1, 0).astype(BF)
        asked = got[:, wi_rows, :slots].astype(I32).reshape(-1)
        pick = (asked[:, None] == jnp.arange(cache.shape[0], dtype=I32)).astype(BF)
        served = dot(pick, table, 1, 0).astype(BF).reshape(owners, slots, width)
        fetched = lax.all_to_all(served, ("z", "y"), split_axis=0, concat_axis=0, tiled=True)
        mine = pl.pallas_call(
            unsort_kernel,
            out_shape=jax.ShapeDtypeStruct((members * pairs, width), BF),
            in_specs=[VMEM, VMEM],
            out_specs=VMEM,
            compiler_params=SMALL,
        )(slot, fetched.reshape(owners * slots, width))

        image_pieces = whole_group(mine)
        images = members * pairs
        img = pl.pallas_call(
            functools.partial(image_kernel, members, nc),
            out_shape=jax.ShapeDtypeStruct((images, emb), BF),
            in_specs=[SMEM] + [ANY] * members,
            out_specs=VMEM,
            scratch_shapes=[pltpu.VMEM((images, emb), BF), pltpu.SemaphoreType.DMA((members,))],
            compiler_params=SMALL,
        )(me.reshape(1), *image_pieces)
        out = pl.pallas_call(
            functools.partial(grad_kernel, rows),
            out_shape=jax.ShapeDtypeStruct((pairs, d_txt), BF),
            in_specs=[SMEM, SMEM, SMEM] + [VMEM] * 4,
            out_specs=VMEM,
            scratch_shapes=[pltpu.VMEM((images, pairs), BF)],
            compiler_params=SMALL,
            cost_estimate=pl.CostEstimate(
                flops=4 * pairs * d_txt * emb, bytes_accessed=2 * d_txt * emb, transcendentals=0
            ),
        )(me.reshape(1), stretch, offset, info, text.reshape(pairs, d_txt), wt_all, img)
        return out.reshape(micro, rows, d_txt)

    return local


def solution(mesh):
    nz, ny, nx, nc = 8, 8, 4, 2
    fine = Mesh(mesh.devices.reshape(nz, ny, nx, nc), ("z", "y", "x", "core"))
    dp, every = ("z", "y"), ("z", "y", "x", "core")
    return jax.shard_map(
        make_local(nz, ny, nx, nc),
        mesh=fine,
        in_specs=(
            P(None, every, None),
            P(dp, None),
            P(None, every, None),
            P(None, every),
            P(None, every),
            P(dp, None),
            P(dp, None),
            P(),
            P(),
        ),
        out_specs=P(None, every, None),
        check_vma=False,
    )
```

```python
import functools

import jax
import jax.numpy as jnp
from jax import lax
from jax.experimental import pallas as pl
from jax.experimental.pallas import tpu as pltpu
from jax.sharding import Mesh, PartitionSpec as P

EPS = 1e-06
LOSS_SCALE = 256.0
CAP = 2
HOPS = (0, 1, 3, 2)
LANES = 128
BF = jnp.bfloat16
F32 = jnp.float32
I32 = jnp.int32
VMEM = pl.BlockSpec(memory_space=pltpu.VMEM)
SMEM = pl.BlockSpec(memory_space=pltpu.SMEM)
ANY = pl.BlockSpec(memory_space=pl.ANY)
SMALL = pltpu.CompilerParams(vmem_limit_bytes=16 * 1024 * 1024)
LAST = pltpu.CompilerParams(vmem_limit_bytes=48 * 1024 * 1024)
LARGE = pltpu.CompilerParams(vmem_limit_bytes=58 * 1024 * 1024)


def dot(a, b, left, right):
    return lax.dot_general(a, b, (((left,), (right,)), ((), ())), preferred_element_type=F32)


def iota(shape, dim):
    return lax.broadcasted_iota(I32, shape, dim)


def as_column(row):
    return jnp.broadcast_to(row, (row.shape[1], row.shape[1])).T


def pack_kernel(owner, entry, labels, info):
    micro = owner.shape[0]
    lines = [
        [owner[m] for m in range(micro)],
        [entry[m:m + 1, :] for m in range(micro)],
        [labels[m:m + 1, :] for m in range(micro)],
    ]
    for k, line in enumerate(lines):
        line = jnp.concatenate(line, axis=1)
        for g in range(info.shape[0]):
            info[g, k:k + 1, :] = line


def ask_kernel(micro, rows, owners, info, ask, slot):
    members = info.shape[0]
    pairs, slots = micro * rows, members * micro * CAP
    r, c = iota((pairs, pairs), 0), iota((pairs, pairs), 1)
    before = ((r < c) & ((r >= rows) == (c >= rows))).astype(F32).astype(BF)
    owner_id, slot_id = iota((owners, pairs), 0), iota((LANES, pairs), 0)
    half = (iota((1, pairs), 1) >= rows).astype(I32) * CAP
    total = jnp.zeros((owners, LANES), F32)
    for g in range(members):
        own, pos = info[g, 0:1, :], info[g, 1:2, :]
        hit = own == owner_id
        hits = hit.astype(F32)
        earlier = dot(hits.astype(BF), before, 1, 0)
        nth = jnp.sum(hits * earlier, axis=0, keepdims=True).astype(I32)
        place = g * micro * CAP + half + nth
        slot[g:g + 1, :] = own * slots + place
        put = jnp.where(place == slot_id, pos, 0).astype(F32).astype(BF)
        total = total + dot(hits.astype(BF), put, 1, 1)
    ask[...] = total.astype(BF)


def unsort_kernel(slot, fetched, mine):
    members, pairs = slot.shape
    count = fetched.shape[0]
    lane = iota((pairs, count), 1)
    for g in range(members):
        column = as_column(slot[g:g + 1, :])
        where = (lane == jnp.concatenate([column] * (count // pairs), axis=1)).astype(F32).astype(BF)
        mine[g * pairs:(g + 1) * pairs, :] = dot(where, fetched[...], 1, 0).astype(BF)


def load_columns(me, cores, pieces, whole, sems):
    chips, width = len(pieces) // cores, whole.shape[1] // len(pieces)
    x, core = me // cores, me % cores
    copies = []
    for k, piece in enumerate(pieces):
        member = (x + chips - HOPS[k % chips]) % chips * cores + (core ^ (k // chips))
        columns = pl.ds(pl.multiple_of(member * width, LANES), width)
        copies.append(pltpu.make_async_copy(piece, whole.at[:, columns], sems.at[k]))
    for copy in copies:
        copy.start()
    return copies


def image_kernel(members, cores, me, *refs):
    images, (img, raw, sems) = refs[:members], refs[members:]
    for copy in load_columns(me[0], cores, images, raw, sems):
        copy.wait()
    for g in range(members):
        span = slice(g * LANES, (g + 1) * LANES)
        wide = raw[span, :].astype(F32)
        inv = lax.rsqrt(jnp.sum(wide * wide, axis=1, keepdims=True) + EPS)
        img[span, :] = (wide * inv).astype(BF)


def grad_kernel(rows, me, stretch, shift, info, text, img, weights, out, wt, slopes, sems):
    chunk = wt.shape[0] // sems.shape[0]
    spans = [slice(k * chunk, (k + 1) * chunk) for k in range(sems.shape[0])]
    copies = [pltpu.make_async_copy(weights.at[p], wt.at[p], sems.at[k]) for k, p in enumerate(spans)]
    for copy in copies:
        copy.start()
    gain, offset = stretch[0], shift[0]
    pairs = text.shape[0]
    same_micro = (iota((pairs, pairs), 0) >= rows) == (iota((pairs, pairs), 1) >= rows)
    own_labels = info[me[0], 2:3, :]
    raw = jnp.zeros((pairs, wt.shape[1]), F32)
    for copy, span in zip(copies, spans):
        copy.wait()
        raw = raw + dot(text[:, span], wt[span, :], 1, 0)
    inverse = lax.rsqrt(jnp.sum(raw * raw, axis=1, keepdims=True) + EPS)
    unit = raw * inverse
    unit_bf = unit.astype(BF)
    for g in range(img.shape[0] // pairs):
        span = slice(g * pairs, (g + 1) * pairs)
        match = (as_column(info[g, 2:3, :]) == own_labels).astype(F32)
        logit = gain * dot(img[span, :], unit_bf, 1, 1) + offset
        slope = LOSS_SCALE * (jax.nn.sigmoid(logit) - match)
        slopes[span, :] = jnp.where(same_micro, slope, 0.0).astype(BF)
    grad = gain * dot(slopes[...], img[...], 0, 0)
    grad = grad - unit * jnp.sum(unit * grad, axis=1, keepdims=True)
    grad = (inverse * grad).astype(BF)
    out[...] = dot(grad, wt[...], 1, 1).astype(BF)


def make_local(nz, ny, nx, nc):
    members, owners = nx * nc, nz * ny

    def swap(v):
        return lax.ppermute(v, "core", [(i, nc - 1 - i) for i in range(nc)])

    def shift(v, by):
        return lax.ppermute(v, "x", [(i, (i + by) % nx) for i in range(nx)])

    def whole_group(v):
        near = [v] + [shift(v, hop) for hop in HOPS[1:]]
        return near + [swap(p) for p in near]

    def local(text, cache, owner, entry, labels, wi, wt, stretch, offset):
        micro, rows, d_txt = text.shape
        d_img, emb = cache.shape[1], wi.shape[1]
        wi_rows, wt_rows = wi.shape[0], wt.shape[0]
        width = emb // members
        pairs = micro * rows
        slots = members * micro * CAP
        x, core = lax.axis_index("x"), lax.axis_index("core")
        me = x * nc + core

        wt_all = lax.all_gather(wt, ("z", "y"), axis=0, tiled=True)

        info = pl.pallas_call(
            pack_kernel,
            out_shape=jax.ShapeDtypeStruct((members, 3, pairs), I32),
            in_specs=[VMEM, VMEM, VMEM],
            out_specs=VMEM,
            compiler_params=LARGE,
        )(owner.transpose(0, 2, 1), entry, labels)
        info = lax.all_to_all(info, ("x", "core"), split_axis=0, concat_axis=0, tiled=True)
        ask, slot = pl.pallas_call(
            functools.partial(ask_kernel, micro, rows, owners),
            out_shape=(
                jax.ShapeDtypeStruct((owners, LANES), BF),
                jax.ShapeDtypeStruct((members, pairs), I32),
            ),
            in_specs=[VMEM],
            out_specs=(VMEM, VMEM),
            compiler_params=SMALL,
        )(info)

        wi_pad = -(-(wi_rows + 1) // 8) * 8
        wi_part = lax.dynamic_slice(wi, (0, me * width), (wi_rows, width))
        sent = jnp.concatenate(
            [
                jnp.broadcast_to(wi_part[None], (owners,) + wi_part.shape),
                ask[:, None, :],
                jnp.zeros((owners, wi_pad - wi_rows - 1, width), BF),
            ],
            axis=1,
        )
        got = lax.all_to_all(sent, ("z", "y"), split_axis=0, concat_axis=0, tiled=True)

        old, new = iota((d_img, owners * wi_pad), 0), iota((d_img, owners * wi_pad), 1)
        spread = (old // wi_rows * wi_pad + old % wi_rows == new).astype(BF)
        cache_pad = dot(cache, spread, 1, 0).astype(BF)
        wi_all = got.reshape(owners * wi_pad, width)
        table = dot(cache_pad, wi_all, 1, 0).astype(BF)
        asked = got[:, wi_rows, :slots].astype(I32).reshape(-1)
        pick = (asked[:, None] == jnp.arange(cache.shape[0], dtype=I32)).astype(BF)
        served = dot(pick, table, 1, 0).astype(BF).reshape(owners, slots, width)
        fetched = lax.all_to_all(served, ("z", "y"), split_axis=0, concat_axis=0, tiled=True)
        mine = pl.pallas_call(
            unsort_kernel,
            out_shape=jax.ShapeDtypeStruct((members * pairs, width), BF),
            in_specs=[VMEM, VMEM],
            out_specs=VMEM,
            compiler_params=SMALL,
        )(slot, fetched.reshape(owners * slots, width))

        image_pieces = whole_group(mine)
        images = members * pairs
        img = pl.pallas_call(
            functools.partial(image_kernel, members, nc),
            out_shape=jax.ShapeDtypeStruct((images, emb), BF),
            in_specs=[SMEM] + [ANY] * members,
            out_specs=VMEM,
            scratch_shapes=[pltpu.VMEM((images, emb), BF), pltpu.SemaphoreType.DMA((members,))],
            compiler_params=SMALL,
        )(me.reshape(1), *image_pieces)
        out = pl.pallas_call(
            functools.partial(grad_kernel, rows),
            out_shape=jax.ShapeDtypeStruct((pairs, d_txt), BF),
            in_specs=[SMEM, SMEM, SMEM] + [VMEM] * 3 + [ANY],
            out_specs=VMEM,
            scratch_shapes=[
                pltpu.VMEM((d_txt, emb), BF),
                pltpu.VMEM((images, pairs), BF),
                pltpu.SemaphoreType.DMA((4,)),
            ],
            compiler_params=LAST,
            cost_estimate=pl.CostEstimate(
                flops=4 * pairs * d_txt * emb, bytes_accessed=2 * d_txt * emb, transcendentals=0
            ),
        )(me.reshape(1), stretch, offset, info, text.reshape(pairs, d_txt), img, wt_all)
        return out.reshape(micro, rows, d_txt)

    return local


def solution(mesh):
    nz, ny, nx, nc = 8, 8, 4, 2
    fine = Mesh(mesh.devices.reshape(nz, ny, nx, nc), ("z", "y", "x", "core"))
    dp, every = ("z", "y"), ("z", "y", "x", "core")
    return jax.shard_map(
        make_local(nz, ny, nx, nc),
        mesh=fine,
        in_specs=(
            P(None, every, None),
            P(dp, None),
            P(None, every, None),
            P(None, every),
            P(None, every),
            P(dp, None),
            P(dp, None),
            P(),
            P(),
        ),
        out_specs=P(None, every, None),
        check_vma=False,
    )
```

```python
import functools

import jax
import jax.numpy as jnp
from jax import lax
from jax.experimental import pallas as pl
from jax.experimental.pallas import tpu as pltpu
from jax.sharding import Mesh, PartitionSpec as P

EPS = 1e-06
LOSS_SCALE = 256.0
CAP = 2
HOPS = (0, 1, 3, 2)
LANES = 128
BF = jnp.bfloat16
F32 = jnp.float32
I32 = jnp.int32
VMEM = pl.BlockSpec(memory_space=pltpu.VMEM)
SMEM = pl.BlockSpec(memory_space=pltpu.SMEM)
ANY = pl.BlockSpec(memory_space=pl.ANY)
SMALL = pltpu.CompilerParams(vmem_limit_bytes=16 * 1024 * 1024)
LAST = pltpu.CompilerParams(vmem_limit_bytes=48 * 1024 * 1024)
LARGE = pltpu.CompilerParams(vmem_limit_bytes=58 * 1024 * 1024)


def dot(a, b, left, right):
    return lax.dot_general(a, b, (((left,), (right,)), ((), ())), preferred_element_type=F32)


def iota(shape, dim):
    return lax.broadcasted_iota(I32, shape, dim)


def as_column(row):
    return jnp.broadcast_to(row, (row.shape[1], row.shape[1])).T


def pack_kernel(owner, entry, labels, info):
    micro = owner.shape[0]
    lines = [
        [owner[m] for m in range(micro)],
        [entry[m:m + 1, :] for m in range(micro)],
        [labels[m:m + 1, :] for m in range(micro)],
    ]
    for k, line in enumerate(lines):
        line = jnp.concatenate(line, axis=1)
        for g in range(info.shape[0]):
            info[g, k:k + 1, :] = line


def ask_kernel(micro, rows, owners, info, ask, slot):
    members = info.shape[0]
    pairs, slots = micro * rows, members * micro * CAP
    r, c = iota((pairs, pairs), 0), iota((pairs, pairs), 1)
    before = ((r < c) & ((r >= rows) == (c >= rows))).astype(F32).astype(BF)
    owner_id, slot_id = iota((owners, pairs), 0), iota((LANES, pairs), 0)
    half = (iota((1, pairs), 1) >= rows).astype(I32) * CAP
    total = jnp.zeros((owners, LANES), F32)
    for g in range(members):
        own, pos = info[g, 0:1, :], info[g, 1:2, :]
        hit = own == owner_id
        hits = hit.astype(F32)
        earlier = dot(hits.astype(BF), before, 1, 0)
        nth = jnp.sum(hits * earlier, axis=0, keepdims=True).astype(I32)
        place = g * micro * CAP + half + nth
        slot[g:g + 1, :] = own * slots + place
        put = jnp.where(place == slot_id, pos, 0).astype(F32).astype(BF)
        total = total + dot(hits.astype(BF), put, 1, 1)
    ask[...] = total.astype(BF)


def unsort_kernel(slot, fetched, mine):
    members, pairs = slot.shape
    count = fetched.shape[0]
    lane = iota((pairs, count), 1)
    for g in range(members):
        column = as_column(slot[g:g + 1, :])
        where = (lane == jnp.concatenate([column] * (count // pairs), axis=1)).astype(F32).astype(BF)
        mine[g * pairs:(g + 1) * pairs, :] = dot(where, fetched[...], 1, 0).astype(BF)


def load_columns(me, cores, pieces, whole, sems):
    chips, width = len(pieces) // cores, whole.shape[1] // len(pieces)
    x, core = me // cores, me % cores
    copies = []
    for k, piece in enumerate(pieces):
        member = (x + chips - HOPS[k % chips]) % chips * cores + (core ^ (k // chips))
        columns = pl.ds(pl.multiple_of(member * width, LANES), width)
        copies.append(pltpu.make_async_copy(piece, whole.at[:, columns], sems.at[k]))
    for copy in copies:
        copy.start()
    return copies


def image_kernel(members, cores, me, *refs):
    images, (img, raw, sems) = refs[:members], refs[members:]
    for copy in load_columns(me[0], cores, images, raw, sems):
        copy.wait()
    for g in range(members):
        span = slice(g * LANES, (g + 1) * LANES)
        wide = raw[span, :].astype(F32)
        inv = lax.rsqrt(jnp.sum(wide * wide, axis=1, keepdims=True) + EPS)
        img[span, :] = (wide * inv).astype(BF)


def grad_kernel(rows, me, stretch, shift, info, text, img, weights, out, wt, slopes, sems):
    chunk = wt.shape[0] // sems.shape[0]
    spans = [slice(k * chunk, (k + 1) * chunk) for k in range(sems.shape[0])]
    copies = [pltpu.make_async_copy(weights.at[p], wt.at[p], sems.at[k]) for k, p in enumerate(spans)]
    for copy in copies:
        copy.start()
    gain, offset = stretch[0], shift[0]
    pairs = text.shape[0]
    same_micro = (iota((pairs, pairs), 0) >= rows) == (iota((pairs, pairs), 1) >= rows)
    own_labels = as_column(info[me[0], 2:3, :])
    raw = jnp.zeros((pairs, wt.shape[1]), F32)
    for copy, span in zip(copies, spans):
        copy.wait()
        raw = raw + dot(text[:, span], wt[span, :], 1, 0)
    inverse = lax.rsqrt(jnp.sum(raw * raw, axis=1, keepdims=True) + EPS)
    unit = raw * inverse
    unit_bf = unit.astype(BF)
    similar = dot(unit_bf, img[...], 1, 1)
    for g in range(img.shape[0] // pairs):
        span = slice(g * pairs, (g + 1) * pairs)
        match = (own_labels == info[g, 2:3, :]).astype(F32)
        slope = LOSS_SCALE * (jax.nn.sigmoid(gain * similar[:, span] + offset) - match)
        slopes[:, span] = jnp.where(same_micro, slope, 0.0).astype(BF)
    grad = gain * dot(slopes[...], img[...], 1, 0)
    grad = grad - unit * jnp.sum(unit * grad, axis=1, keepdims=True)
    grad = (inverse * grad).astype(BF)
    out[...] = dot(grad, wt[...], 1, 1).astype(BF)


def make_local(nz, ny, nx, nc):
    members, owners = nx * nc, nz * ny

    def swap(v):
        return lax.ppermute(v, "core", [(i, nc - 1 - i) for i in range(nc)])

    def shift(v, by):
        return lax.ppermute(v, "x", [(i, (i + by) % nx) for i in range(nx)])

    def whole_group(v):
        near = [v] + [shift(v, hop) for hop in HOPS[1:]]
        return near + [swap(p) for p in near]

    def local(text, cache, owner, entry, labels, wi, wt, stretch, offset):
        micro, rows, d_txt = text.shape
        d_img, emb = cache.shape[1], wi.shape[1]
        wi_rows, wt_rows = wi.shape[0], wt.shape[0]
        width = emb // members
        pairs = micro * rows
        slots = members * micro * CAP
        x, core = lax.axis_index("x"), lax.axis_index("core")
        me = x * nc + core

        wt_all = lax.all_gather(wt, ("z", "y"), axis=0, tiled=True)

        info = pl.pallas_call(
            pack_kernel,
            out_shape=jax.ShapeDtypeStruct((members, 3, pairs), I32),
            in_specs=[VMEM, VMEM, VMEM],
            out_specs=VMEM,
            compiler_params=LARGE,
        )(owner.transpose(0, 2, 1), entry, labels)
        info = lax.all_to_all(info, ("x", "core"), split_axis=0, concat_axis=0, tiled=True)
        ask, slot = pl.pallas_call(
            functools.partial(ask_kernel, micro, rows, owners),
            out_shape=(
                jax.ShapeDtypeStruct((owners, LANES), BF),
                jax.ShapeDtypeStruct((members, pairs), I32),
            ),
            in_specs=[VMEM],
            out_specs=(VMEM, VMEM),
            compiler_params=SMALL,
        )(info)

        wi_pad = -(-(wi_rows + 1) // 8) * 8
        wi_part = lax.dynamic_slice(wi, (0, me * width), (wi_rows, width))
        sent = jnp.concatenate(
            [
                jnp.broadcast_to(wi_part[None], (owners,) + wi_part.shape),
                ask[:, None, :],
                jnp.zeros((owners, wi_pad - wi_rows - 1, width), BF),
            ],
            axis=1,
        )
        got = lax.all_to_all(sent, ("z", "y"), split_axis=0, concat_axis=0, tiled=True)

        old, new = iota((d_img, owners * wi_pad), 0), iota((d_img, owners * wi_pad), 1)
        spread = (old // wi_rows * wi_pad + old % wi_rows == new).astype(BF)
        cache_pad = dot(cache, spread, 1, 0).astype(BF)
        wi_all = got.reshape(owners * wi_pad, width)
        table = dot(cache_pad, wi_all, 1, 0).astype(BF)
        asked = got[:, wi_rows, :slots].astype(I32).reshape(-1)
        pick = (asked[:, None] == jnp.arange(cache.shape[0], dtype=I32)).astype(BF)
        served = dot(pick, table, 1, 0).astype(BF).reshape(owners, slots, width)
        fetched = lax.all_to_all(served, ("z", "y"), split_axis=0, concat_axis=0, tiled=True)
        mine = pl.pallas_call(
            unsort_kernel,
            out_shape=jax.ShapeDtypeStruct((members * pairs, width), BF),
            in_specs=[VMEM, VMEM],
            out_specs=VMEM,
            compiler_params=SMALL,
        )(slot, fetched.reshape(owners * slots, width))

        image_pieces = whole_group(mine)
        images = members * pairs
        img = pl.pallas_call(
            functools.partial(image_kernel, members, nc),
            out_shape=jax.ShapeDtypeStruct((images, emb), BF),
            in_specs=[SMEM] + [ANY] * members,
            out_specs=VMEM,
            scratch_shapes=[pltpu.VMEM((images, emb), BF), pltpu.SemaphoreType.DMA((members,))],
            compiler_params=SMALL,
        )(me.reshape(1), *image_pieces)
        out = pl.pallas_call(
            functools.partial(grad_kernel, rows),
            out_shape=jax.ShapeDtypeStruct((pairs, d_txt), BF),
            in_specs=[SMEM, SMEM, SMEM] + [VMEM] * 3 + [ANY],
            out_specs=VMEM,
            scratch_shapes=[
                pltpu.VMEM((d_txt, emb), BF),
                pltpu.VMEM((pairs, images), BF),
                pltpu.SemaphoreType.DMA((4,)),
            ],
            compiler_params=LAST,
            cost_estimate=pl.CostEstimate(
                flops=4 * pairs * d_txt * emb, bytes_accessed=2 * d_txt * emb, transcendentals=0
            ),
        )(me.reshape(1), stretch, offset, info, text.reshape(pairs, d_txt), img, wt_all)
        return out.reshape(micro, rows, d_txt)

    return local


def solution(mesh):
    nz, ny, nx, nc = 8, 8, 4, 2
    fine = Mesh(mesh.devices.reshape(nz, ny, nx, nc), ("z", "y", "x", "core"))
    dp, every = ("z", "y"), ("z", "y", "x", "core")
    return jax.shard_map(
        make_local(nz, ny, nx, nc),
        mesh=fine,
        in_specs=(
            P(None, every, None),
            P(dp, None),
            P(None, every, None),
            P(None, every),
            P(None, every),
            P(dp, None),
            P(dp, None),
            P(),
            P(),
        ),
        out_specs=P(None, every, None),
        check_vma=False,
    )
```
